32 devices in a mesh: dom: 8 (over z, x), row: 4 (over y, core).
Axes of the slice: x: 2, y: 2, z: 4, core: 2. Of those that a mesh axis runs over, the one named last changes fastest.
Arguments:
- features: bfloat16 [16384, 2048], P(('dom', 'row')), may hold values from -6 to 6
- adjacency: bfloat16 [16384, 2048], P(('dom', 'row')), as said below
- tile_values: bfloat16 [2048, 128, 128], P(('dom', 'row')), as said below
- tile_block: int32 [2048], P(('dom', 'row')), may hold values from 0 to 3
- tile_slot: int32 [2048], P(('dom', 'row')), may hold values from 0 to 7, as said below
- tile_count: int32 [32], P(('dom', 'row')), may hold values from 16 to 64
- send_block: int32 [32, 8], P(('dom', 'row')), may hold values from -1 to 3, as said below
- node_mask: int32 [16384], P(('dom', 'row')), may hold values from 0 to 1, as said below
- weight: float32 [2048, 2048], P('row')
- params: float32 [3, 2048], replicated
- weight_first: float32 [2048, 2048], P('row')
- weight_second: float32 [2048, 2048], P('row'), as said below
- params_first: float32 [3, 2048], replicated
- params_second: float32 [3, 2048], replicated, as said below
- cotangent: bfloat16 [16384, 2048], P(('dom', 'row')), may hold values from -6 to 6
Outputs:
- output: bfloat16 [16384, 2048], P(('dom', 'row'))
- grad_features: bfloat16 [16384, 2048], P(('dom', 'row'))
- weight_new: float32 [2048, 2048], P('row')
- weight_low: bfloat16 [2048, 2048], P('row')
- weight_first_new: float32 [2048, 2048], P('row')
- weight_second_new: float32 [2048, 2048], P('row')
- params_new: float32 [3, 2048], replicated
- params_first_new: float32 [3, 2048], replicated
- params_second_new: float32 [3, 2048], replicated
- norms: float32 [4, 2], replicated
The draws below stay inside these ranges and needn't reach their ends.
Inputs may be any that keep to these rules, and one draw needn't show every extreme that they name: The adjacency entries are nonnegative; the entry of a node against itself is positive. `tile_values`: the tile entries are nonnegative. `send_block`: entry (p, q) names a row block of device p, or is -1; it is -1 where q is p's own dom index. `tile_slot`: A tile of device (q, r) reads from a dom index d whose device (d, r) sends a block to q. `node_mask`: the first node of every device counts. `weight_second`: second moments are positive. `params_second`: second moments are positive.
All inputs are finite; a program needn't handle non-finite values.
Results may differ from the reference program's by a relative error of at most 0.0081.
Values may be sent and summed in bfloat16 or wider, within the bound.
No kernel may reach another device: no remote copies, remote signals or barrier semaphores. Data moves between devices by JAX's collectives and lax.ppermute only.
A program may use at most 384 MiB of HBM per device.

```python
import math
import jax
import jax.numpy as jnp
from jax import lax

F = 2048
BLOCK = 128
BLOCKS_DEV = 4
STEP = 5
ROWS_DEV = 512
TILES = 64
PART = 2048
NODES = 16384
N_DOM = 8
N_ROW = 4


def links(key):
    device_total = NODES // ROWS_DEV
    peer_total = NODES // PART
    group_size = PART // ROWS_DEV
    key_rate = jax.random.fold_in(key, 101)
    key_roll = jax.random.fold_in(key, 102)
    key_pick = jax.random.fold_in(key, 103)
    sender_rate = jax.random.randint(key_rate, (device_total, 1), 2, 9)
    rolled = jax.random.randint(key_roll, (device_total, peer_total), 0, 8)
    picked = jax.random.randint(key_pick, (device_total, peer_total), 0, BLOCKS_DEV)
    device_ids = jnp.arange(device_total, dtype=jnp.int32)[:, None]
    sender = device_ids // group_size
    target = jnp.arange(peer_total, dtype=jnp.int32)[None, :]
    forced = target == (sender + peer_total - 1) % peer_total
    marked = (device_ids == 0) & (target == 1)
    linked = ((rolled < sender_rate) | forced | marked) & (target != sender)
    picked = jnp.where(marked, BLOCKS_DEV - 1, picked)
    return jnp.where(linked, picked, -1).astype(jnp.int32)


def draw_send_block(key, part):
    sends = links(key)
    return sends


def draw_tile_slot(key, part):
    sends = links(key)
    key = jax.random.fold_in(key, 2)
    device_total = NODES // ROWS_DEV
    peer_total = NODES // PART
    group_size = PART // ROWS_DEV
    arriving = jnp.transpose(sends.reshape(peer_total, group_size, peer_total), (2, 1, 0)).reshape(device_total, peer_total) >= 0
    key_score, key_pick = jax.random.split(key)
    scores = jax.random.randint(key_score, (device_total, peer_total), 0, 1 << 20) * peer_total + jnp.arange(peer_total, dtype=jnp.int32)[None, :]
    ordering = jnp.argsort(jnp.where(arriving, scores, scores + (1 << 28)), axis=1, stable=True).astype(jnp.int32)
    arriving_total = jnp.sum(arriving.astype(jnp.int32), axis=1)
    pick_index = jax.random.randint(key_pick, (device_total, TILES), 0, arriving_total[:, None])
    slots = jnp.take_along_axis(ordering, pick_index, axis=1)
    receiver = jnp.arange(device_total, dtype=jnp.int32) // group_size
    slots = slots.at[:, 0].set((receiver + 1) % peer_total)
    return slots.reshape(device_total * TILES).astype(jnp.int32)


def draw_tile_count(key, part):
    key = jax.random.fold_in(key, 3)
    device_total = NODES // ROWS_DEV
    key_count, key_lucky = jax.random.split(key)
    counts = jax.random.randint(key_count, (device_total,), TILES // 4, TILES + 1)
    lucky = jax.random.randint(key_lucky, (), 0, device_total)
    device_ids = jnp.arange(device_total, dtype=jnp.int32)
    counts = jnp.where(device_ids == lucky, TILES, counts)
    counts = jnp.where(device_ids == (lucky + device_total // 2) % device_total, TILES // 4, counts)
    return counts.astype(jnp.int32)


def sparse_values(key, shape, diagonal):
    key_keep, key_size = jax.random.split(key)
    retained = (jax.random.randint(key_keep, shape, 0, 16) == 0) | diagonal
    magnitude = jax.random.uniform(key_size, shape, jnp.float32, 0.5, 1.5)
    return jnp.where(retained, magnitude * (16.0 / PART), 0.0).astype(jnp.float32)


def draw_tile_values(key, part):
    key = jax.random.fold_in(key, 4)
    shape = (NODES // ROWS_DEV * TILES, BLOCK, BLOCK)
    return sparse_values(key, shape, jnp.zeros(shape, bool)).astype(jnp.bfloat16)


def draw_adjacency(key, part):
    key = jax.random.fold_in(key, 5)
    row_ids = jnp.arange(NODES, dtype=jnp.int32)[:, None]
    col_ids = jnp.arange(PART, dtype=jnp.int32)[None, :]
    return sparse_values(key, (NODES, PART), col_ids == row_ids % PART).astype(jnp.bfloat16)


def draw_node_mask(key, part):
    key = jax.random.fold_in(key, 6)
    peer_total = NODES // PART
    group_size = PART // ROWS_DEV
    row_ids = jnp.arange(NODES, dtype=jnp.int32)
    device = row_ids // ROWS_DEV
    spread = peer_total + group_size
    barrier = spread + 2 * (device // group_size) + 2 * (device % group_size)
    score = jax.random.randint(key, (NODES,), 0, 3 * spread)
    counted = (score < barrier) | (row_ids % ROWS_DEV == 0)
    counted = counted & (row_ids != 1)
    return counted.astype(jnp.int32)


def rising(count, length):
    position = jnp.arange(count, dtype=jnp.float32) / length
    return 1.0 + 0.75 * position


def signed(key, shape):
    return jnp.clip(jax.random.normal(key, shape, jnp.float32), -6.0, 6.0)


def positive(key, shape):
    return jnp.exp(jax.random.uniform(key, shape, jnp.float32, 0.0, math.log(4.0)))


def draw_weight(key, part):
    key = jax.random.fold_in(key, 7)
    return signed(key, (F, F)) * rising(F, F)[:, None] * math.sqrt(PART / (32.0 * F))


def draw_params(key, part):
    key = jax.random.fold_in(key, 8)
    key_bias, key_scale, key_shift = jax.random.split(key, 3)
    lift = rising(F, F)
    bias = 0.5 * signed(key_bias, (F,)) * lift
    scale = jax.random.uniform(key_scale, (F,), jnp.float32, 0.5, 1.5) * lift
    shift = 0.5 * signed(key_shift, (F,)) * lift
    return jnp.stack([bias, scale, shift]).astype(jnp.float32)


def draw_weight_first(key, part):
    key = jax.random.fold_in(key, 9)
    return signed(key, (F, F)) * (0.8 * math.sqrt(32.0 * NODES / PART))


def draw_weight_second(key, part):
    key = jax.random.fold_in(key, 10)
    return positive(key, (F, F)) * (0.64 * 32.0 * NODES / PART)


def draw_params_first(key, part):
    key = jax.random.fold_in(key, 11)
    return signed(key, (3, F)) * (0.75 * math.sqrt(NODES))


def draw_params_second(key, part):
    key = jax.random.fold_in(key, 12)
    return positive(key, (3, F)) * (0.5625 * NODES)


def plant(entries, rng, low, largest):
    shape = entries.shape
    spot = [jax.random.randint(jax.random.fold_in(rng, axis), (), 0, shape[axis]) for axis in range(len(shape))]
    entries = entries.at[tuple(spot)].set(low)
    longest = shape.index(max(shape))
    spot[longest] = (spot[longest] + 1) % shape[longest]
    return entries.at[tuple(spot)].set(largest)


def block_scale(own_key, dims, cuts, low, top_value):
    level = 1.0
    for axis_at, parts in cuts:
        heights = jax.random.uniform(jax.random.fold_in(jax.random.fold_in(own_key, 6), axis_at), (parts,), jnp.float32, low / len(cuts), top_value / len(cuts))
        level = level * jnp.repeat(jnp.exp(heights), dims[axis_at] // parts).reshape((-1,) + (1,) * (len(dims) - 1 - axis_at))
    return level


def gaussian(own_key, dims, scale, reach, pieces=(), kind=jnp.bfloat16):
    loudness = block_scale(own_key, dims, pieces, -0.22, 0.18) if pieces else 1.0
    result = jax.random.normal(own_key, dims, jnp.float32) * scale * loudness
    return jnp.minimum(jnp.maximum(result, -reach), reach).astype(kind)


def setup_inputs(seed: int = 0) -> dict:
    keys = jax.random.split(jax.random.key(seed), 16)
    features = gaussian(keys[0], (NODES, F), 1.0, 6.0, ((0, 32),))
    adjacency = draw_adjacency(jax.random.fold_in(keys[15], 71), 0)
    tile_values = draw_tile_values(jax.random.fold_in(keys[15], 71), 0)
    tile_block = plant(jax.random.randint(keys[3], (N_DOM * N_ROW * TILES,), 0, BLOCKS_DEV), jax.random.fold_in(keys[3], 1), 0, BLOCKS_DEV - 1).astype(jnp.int32)
    tile_slot = draw_tile_slot(jax.random.fold_in(keys[15], 71), 0)
    tile_count = draw_tile_count(jax.random.fold_in(keys[15], 71), 0)
    send_block = draw_send_block(jax.random.fold_in(keys[15], 71), 0)
    node_mask = draw_node_mask(jax.random.fold_in(keys[15], 71), 0)
    weight = draw_weight(jax.random.fold_in(keys[15], 71), 0)
    params = draw_params(jax.random.fold_in(keys[15], 71), 0)
    weight_first = draw_weight_first(jax.random.fold_in(keys[15], 71), 0)
    weight_second = draw_weight_second(jax.random.fold_in(keys[15], 71), 0)
    params_first = draw_params_first(jax.random.fold_in(keys[15], 71), 0)
    params_second = draw_params_second(jax.random.fold_in(keys[15], 71), 0)
    cotangent = gaussian(keys[14], (NODES, F), 1.0, 6.0, ((0, 32),))
    return {"features": features, "adjacency": adjacency, "tile_values": tile_values, "tile_block": tile_block, "tile_slot": tile_slot, "tile_count": tile_count, "send_block": send_block, "node_mask": node_mask, "weight": weight, "params": params, "weight_first": weight_first, "weight_second": weight_second, "params_first": params_first, "params_second": params_second, "cotangent": cotangent}


@jax.custom_vjp
def low(v):
    return lax.optimization_barrier(v.astype(jnp.bfloat16)).astype(jnp.float32)

@jax.custom_vjp
def low_back(v):
    return v

def low_keep(v):
    return (low(v), None)

def low_pass(kept, grad):
    return (grad,)

def back_keep(v):
    return (v, None)

def back_low(kept, grad):
    return (low(grad),)
low.defvjp(low_keep, low_pass)
low_back.defvjp(back_keep, back_low)
PRECISE = lax.Precision.HIGHEST
SELF_LOOP = 1.0
NORM_EPS = 1e-05
DECAY_FIRST = 0.5
DECAY_SECOND = 0.5
ADAM_EPS = 1e-06
WEIGHT_DECAY = 0.01
LEARN_RATE = 0.5
TRUST_EPS = 1e-06

def aggregate(float_features, adjacency, tile_values, tile_block, tile_slot, tile_count, send_block):
    device_total = N_DOM * N_ROW
    part_blocks = float_features.reshape(N_DOM, N_ROW, BLOCKS_DEV, BLOCK, F)
    sends = send_block.reshape(N_DOM, N_ROW, N_DOM)
    adj_rows = adjacency.astype(jnp.float32).reshape(device_total, ROWS_DEV, PART)
    tile_float = tile_values.astype(jnp.float32).reshape(device_total, TILES, BLOCK, BLOCK)
    block_table = tile_block.reshape(device_total, TILES)
    slot_table = tile_slot.reshape(device_total, TILES)
    block_ids = jnp.arange(BLOCKS_DEV, dtype=jnp.int32)
    tile_ids = jnp.arange(TILES, dtype=jnp.int32)

    @jax.checkpoint
    def device_rows(index):
        group = index // N_ROW
        member = index % N_ROW
        own_part = part_blocks[group].reshape(PART, F)
        my_adjacency = adj_rows[index]
        intra = jnp.dot(my_adjacency, own_part, precision=PRECISE)
        own_rows = lax.dynamic_slice_in_dim(own_part, member * ROWS_DEV, ROWS_DEV, 0)
        diagonal = jnp.diagonal(lax.dynamic_slice_in_dim(my_adjacency, member * ROWS_DEV, ROWS_DEV, 1))
        sources = part_blocks[:, member]
        picks = sends[:, member, group]
        chooser = (picks[:, None] == block_ids[None, :]).astype(jnp.float32)
        received = low_back(jnp.einsum('db,dbkf->dkf', chooser, sources, precision=PRECISE))
        live_mask = (tile_ids < tile_count[index]).astype(jnp.float32)
        picked = received[slot_table[index]]
        products = jnp.einsum('tij,tjf->tif', tile_float[index], picked, precision=PRECISE) * live_mask[:, None, None]
        halo_sum = jnp.zeros((BLOCKS_DEV, BLOCK, F), jnp.float32).at[block_table[index]].add(products)
        return intra + SELF_LOOP * diagonal[:, None] * own_rows + halo_sum.reshape(ROWS_DEV, F)
    return lax.map(device_rows, jnp.arange(device_total, dtype=jnp.int32)).reshape(NODES, F)

def lamb(value, grad, first, second, decay, axis):
    first_new = DECAY_FIRST * first + (1.0 - DECAY_FIRST) * grad
    second_new = DECAY_SECOND * second + (1.0 - DECAY_SECOND) * grad * grad
    update = first_new / (1.0 - DECAY_FIRST ** STEP) / (jnp.sqrt(second_new / (1.0 - DECAY_SECOND ** STEP)) + ADAM_EPS) + decay * value
    value_norm = jnp.sqrt(lax.optimization_barrier(jnp.sum(value * value, axis=axis, keepdims=True)))
    update_norm = jnp.sqrt(lax.optimization_barrier(jnp.sum(update * update, axis=axis, keepdims=True)))
    new_value = value - LEARN_RATE * (value_norm / (update_norm + TRUST_EPS)) * update
    return (new_value, first_new, second_new, value_norm, update_norm)

def reference(features, adjacency, tile_values, tile_block, tile_slot, tile_count, send_block, node_mask, weight, params, weight_first, weight_second, params_first, params_second, cotangent):
    mask_col = node_mask.astype(jnp.float32)[:, None]

    def forward(float_features, float_weight, float_params):
        summed = aggregate(float_features, adjacency, tile_values, tile_block, tile_slot, tile_count, send_block)
        hidden = low(low_back(summed))
        preact = low_back(jnp.dot(hidden, low(float_weight), precision=PRECISE) + float_params[0])
        activated = jax.nn.gelu(preact)
        node_count = jnp.sum(mask_col)
        mean_act = lax.optimization_barrier(jnp.sum(mask_col * activated, axis=0)) / node_count
        centred = activated - mean_act
        variance = lax.optimization_barrier(jnp.sum(mask_col * centred * centred, axis=0)) / node_count
        normed = centred * lax.rsqrt(variance + NORM_EPS)
        return mask_col * (float_params[1] * normed + float_params[2])
    output, pullback = jax.vjp(forward, features.astype(jnp.float32), weight, params)
    grad_features, grad_weight, grad_params = pullback(cotangent.astype(jnp.float32))
    weight_new, weight_first_new, weight_second_new, weight_norm, weight_update_norm = lamb(weight, grad_weight, weight_first, weight_second, WEIGHT_DECAY, None)
    params_new, params_first_new, params_second_new, param_norms, update_norms = lamb(params, grad_params, params_first, params_second, 0.0, 1)
    norms = jnp.concatenate([jnp.concatenate([weight_norm, weight_update_norm], axis=1), jnp.concatenate([param_norms, update_norms], axis=1)], axis=0)
    return (output.astype(jnp.bfloat16), grad_features.astype(jnp.bfloat16), weight_new, weight_new.astype(jnp.bfloat16), weight_first_new, weight_second_new, params_new, params_first_new, params_second_new, norms)
```

```python
import math

import jax
import jax.numpy as jnp
from jax import lax
from jax.experimental import pallas as pl
from jax.experimental.pallas import tpu as pltpu
from jax.sharding import PartitionSpec as P

STEP = 5


SELF_LOOP = 1.0
NORM_EPS = 1e-05
DECAY_FIRST = 0.5
DECAY_SECOND = 0.5
ADAM_EPS = 1e-06
WEIGHT_DECAY = 0.01
LEARN_RATE = 0.5
TRUST_EPS = 1e-06

AXES = ("dom", "row")
GELU_ROOT = math.sqrt(2.0 / math.pi)
GELU_CUBE = 0.044715
STAT_ROWS = 8
GROUP = 8
WEIGHT_PARTS = 2

ANY_ROWS = (((1,), (0,)), ((), ()))
BOTH_LAST = (((1,), (1,)), ((), ()))


def dot(left, right, dims=ANY_ROWS):
    return lax.dot_general(left, right, dims, preferred_element_type=jnp.float32)


def swap(value, dom_flip, row_flip):
    dom_count, row_count = lax.axis_size("dom"), lax.axis_size("row")
    pairs = [
        (d * row_count + r, (d ^ dom_flip) * row_count + (r ^ row_flip))
        for d in range(dom_count)
        for r in range(row_count)
    ]
    return lax.ppermute(value, AXES, pairs)


def call(kernel, *, flops, nbytes, vmem_mb, **kw):
    return pl.pallas_call(
        kernel,
        cost_estimate=pl.CostEstimate(
            flops=int(flops), bytes_accessed=int(nbytes), transcendentals=0
        ),
        compiler_params=pltpu.CompilerParams(vmem_limit_bytes=vmem_mb << 20),
        **kw,
    )


def spread_rows(value):
    near = swap(value, 0, 1)
    far = swap(value, 0, 2)
    return [value, near, far, swap(far, 0, 1)]


def prepare_kernel(
    me, block_ref, slot_ref, count_ref, adj_ref, tile_ref, wide, flip, halo, halo_flip, total
):
    rows = adj_ref.shape[0]
    row_count = adj_ref.shape[1] // rows
    blocks, peers, side = total.shape[0], total.shape[1], total.shape[2]
    for j in range(row_count):
        start = pl.multiple_of((me[1] ^ j) * rows, rows)
        piece = adj_ref[:, pl.ds(start, rows)]
        if j == 0:
            at_row = lax.broadcasted_iota(jnp.int32, (rows, rows), 0)
            at_col = lax.broadcasted_iota(jnp.int32, (rows, rows), 1)
            wide_piece = piece.astype(jnp.float32)
            piece = jnp.where(at_row == at_col, (1.0 + SELF_LOOP) * wide_piece, wide_piece).astype(
                jnp.bfloat16
            )
        wide[:, j * rows : (j + 1) * rows] = piece
        flip[j * rows : (j + 1) * rows, :] = piece.T
    total[...] = jnp.zeros(total.shape, total.dtype)

    def add(t, carry):
        b = block_ref[t]
        k = slot_ref[t] ^ me[0]
        total[b, k] = total[b, k] + tile_ref[t].astype(jnp.float32)
        return carry

    lax.fori_loop(0, count_ref[0], add, 0)
    for b in range(blocks):
        for k in range(peers):
            piece = total[b, k].astype(jnp.bfloat16)
            halo[b * side : (b + 1) * side, k * side : (k + 1) * side] = piece
            halo_flip[k * side : (k + 1) * side, b * side : (b + 1) * side] = piece.T


def prepare(me, tile_block, tile_slot, tile_count, adjacency, tiles, peers):
    rows, part = adjacency.shape
    side = tiles.shape[1]
    smem = pl.BlockSpec(memory_space=pltpu.SMEM)
    vmem = pl.BlockSpec(memory_space=pltpu.VMEM)
    halo_bytes = rows * peers * side * 2
    bf = jnp.bfloat16
    return call(
        prepare_kernel,
        flops=tiles.size,
        nbytes=2 * (adjacency.size * 6 + tiles.size) + 2 * halo_bytes,
        vmem_mb=20 + (4 * halo_bytes >> 20),
        in_specs=[smem] * 4 + [vmem] * 2,
        out_specs=[vmem] * 4,
        out_shape=[
            jax.ShapeDtypeStruct((rows, part), bf),
            jax.ShapeDtypeStruct((part, rows), bf),
            jax.ShapeDtypeStruct((rows, peers * side), bf),
            jax.ShapeDtypeStruct((peers * side, rows), bf),
        ],
        scratch_shapes=[pltpu.VMEM((rows // side, peers, side, side), jnp.float32)],
        name="prepare",
    )(me, tile_block, tile_slot, tile_count, adjacency, tiles)


def gather_kernel(me, wide, halo, *refs):
    hidden, hidden_flip = refs[-2:]
    near = refs[:-2]
    row_count = wide.shape[1] // wide.shape[0]
    side = near[row_count].shape[0]
    total = dot(wide[...], jnp.concatenate([ref[...] for ref in near[:row_count]], axis=0))
    total += dot(halo[:, side:], jnp.concatenate([ref[...] for ref in near[row_count:]], axis=0))
    low = total.astype(jnp.bfloat16)
    hidden[...] = low
    hidden_flip[...] = low.T


def gather(me, wide, halo, own, arrived):
    rows, width = own[0].shape
    row_count = len(own)
    side = arrived[0].shape[0]
    cols = 256
    per = rows // cols

    def place(i, me):
        return ((i // per) ^ me[1]) * per + i % per

    def place_flip(i, me):
        j = (i // per) ^ me[1]
        return ((j % 2) * (row_count // 2) + j // 2) * per + i % per

    whole = lambda shape: pl.BlockSpec(shape, lambda i, me: (0, 0))
    return call(
        gather_kernel,
        flops=2 * rows * width * (row_count * rows + halo.shape[1]),
        nbytes=2 * (wide.size + halo.size + (row_count + 2) * own[0].size + len(arrived) * side * width),
        vmem_mb=24 + (2 * halo.size * 2 + 2 * len(arrived) * side * cols * 4 >> 20),
        grid_spec=pltpu.PrefetchScalarGridSpec(
            num_scalar_prefetch=1,
            grid=(width // cols,),
            in_specs=[whole(wide.shape), whole(halo.shape)]
            + [pl.BlockSpec((rows, cols), lambda i, me: (0, i))] * row_count
            + [pl.BlockSpec((side, cols), lambda i, me: (0, i))] * len(arrived),
            out_specs=[
                pl.BlockSpec((rows, cols), lambda i, me: (0, place(i, me))),
                pl.BlockSpec((cols, rows), lambda i, me: (place_flip(i, me), 0)),
            ],
        ),
        out_shape=[
            jax.ShapeDtypeStruct((rows, width), jnp.bfloat16),
            jax.ShapeDtypeStruct((width, rows), jnp.bfloat16),
        ],
        name="gather",
    )(me, wide, halo, *own, *arrived)


def gelu_parts(v):
    inner = GELU_ROOT * (v + GELU_CUBE * (v * v * v))
    return jnp.tanh(inner)


def linear_kernel(hidden, params, mask_ref, cot_ref, *refs):
    weights, (preact, stats) = refs[:-2], refs[-2:]
    v = dot(hidden[...], jnp.concatenate([ref[...] for ref in weights], axis=0)) + params[0:1, :]
    preact[...] = v
    act = 0.5 * v * (1.0 + gelu_parts(v))
    mask = mask_ref[...]
    count = jnp.sum(mask)
    mean = jnp.sum(mask * act, axis=0, keepdims=True) / count
    centred = act - mean
    grad = mask * cot_ref[...].astype(jnp.float32)
    stats[0:1, :] = mean
    stats[1:2, :] = jnp.sum(mask * centred * centred, axis=0, keepdims=True)
    stats[2:3, :] = jnp.sum(grad, axis=0, keepdims=True)
    stats[3:4, :] = jnp.sum(grad * centred, axis=0, keepdims=True)
    stats[4:8, :] = jnp.full((4, mean.shape[1]), count, jnp.float32)


def linear(hidden, params, mask, cotangent, weights):
    rows, width = hidden.shape
    cols = 256
    wide = pl.BlockSpec((rows, cols), lambda i: (0, i))
    return call(
        linear_kernel,
        flops=2 * rows * width * width,
        nbytes=2 * width * width + 10 * rows * width,
        vmem_mb=28,
        grid=(width // cols,),
        in_specs=[
            pl.BlockSpec((rows, width), lambda i: (0, 0)),
            pl.BlockSpec((3, cols), lambda i: (0, i)),
            pl.BlockSpec((rows, 1), lambda i: (0, 0)),
            wide,
        ]
        + [pl.BlockSpec((w.shape[0], cols), lambda i: (0, i)) for w in weights],
        out_specs=[wide, pl.BlockSpec((STAT_ROWS, cols), lambda i: (0, i))],
        out_shape=[
            jax.ShapeDtypeStruct((rows, width), jnp.float32),
            jax.ShapeDtypeStruct((STAT_ROWS, width), jnp.float32),
        ],
        name="linear",
    )(hidden, params, mask, cotangent, *weights)


def merged(mine, refs, ordered):
    for i, ref in enumerate(refs):
        ordered[mine ^ i] = ref[...]
    parts = [ordered[i] for i in range(len(refs))]
    count = sum(p[4:5] for p in parts)
    mean = sum(p[4:5] * p[0:1] for p in parts) / count
    spread = sum(p[1:2] + p[4:5] * (p[0:1] - mean) * (p[0:1] - mean) for p in parts)
    shift = sum(p[2:3] for p in parts)
    scale = sum(p[3:4] + (p[0:1] - mean) * p[2:3] for p in parts)
    return mean, spread, shift, scale, count


def merge_kernel(mine, *refs):
    out, ordered = refs[-2:]
    for i, row in enumerate(merged(mine[0], refs[:-2], ordered)):
        out[i : i + 1, :] = row
    out[5:8, :] = jnp.zeros((3, out.shape[1]), jnp.float32)


def merge(mine, parts):
    vmem = pl.BlockSpec(memory_space=pltpu.VMEM)
    return call(
        merge_kernel,
        flops=20 * parts[0].size * len(parts),
        nbytes=4 * parts[0].size * len(parts),
        vmem_mb=8,
        in_specs=[pl.BlockSpec(memory_space=pltpu.SMEM)] + [vmem] * len(parts),
        out_specs=vmem,
        out_shape=jax.ShapeDtypeStruct(parts[0].shape, jnp.float32),
        scratch_shapes=[pltpu.VMEM((len(parts),) + parts[0].shape, jnp.float32)],
        name="merge",
    )(mine[None], *parts)


def exchange_stats(stats, dom_at, row_at, dom_count, row_count):
    stats = merge(row_at, [stats] + [swap(stats, 0, j) for j in range(1, row_count)])
    size, step = dom_count, 1
    while size > GROUP:
        parts = [stats] + [swap(stats, step * j, 0) for j in range(1, GROUP)]
        stats = merge((dom_at // step) % GROUP, parts)
        size, step = size // GROUP, step * GROUP
    parts = [stats] + [swap(stats, step * j, 0) for j in range(1, size)]
    return (dom_at // step) % size, parts


def backward_kernel(me, params, mask_ref, cot_ref, pre_ref, *refs, row_count):
    weights = refs[:row_count]
    output, grad_pre, grad_hidden, sums, ordered, total = refs[-6:]
    parts = refs[row_count:-6]
    at = pl.program_id(0)
    rows = weights[0].shape[0]
    mean, spread, shift_grad, scale_sum, count = merged(me[2], parts, ordered)
    inverse = lax.rsqrt(spread / count + NORM_EPS)
    scale_grad = scale_sum * inverse
    v = pre_ref[...]
    mask = mask_ref[...]
    bend = gelu_parts(v)
    act = 0.5 * v * (1.0 + bend)
    normed = (act - mean) * inverse
    scale = params[1:2, :]
    output[...] = (mask * (scale * normed + params[2:3, :])).astype(jnp.bfloat16)
    grad_out = mask * cot_ref[...].astype(jnp.float32)
    grad_act = (
        mask * (scale * inverse) * (grad_out - shift_grad / count - normed * (scale_grad / count))
    )
    slope = 0.5 * (1.0 + bend) + 0.5 * v * (1.0 - bend * bend) * (
        GELU_ROOT * (1.0 + 3.0 * GELU_CUBE * (v * v))
    )
    low = (grad_act * slope).astype(jnp.bfloat16)
    grad_pre[...] = low
    sums[0:1, :] = jnp.sum(low.astype(jnp.float32), axis=0, keepdims=True)
    sums[1:2, :] = scale_grad
    sums[2:3, :] = shift_grad
    sums[3:8, :] = jnp.zeros((5, scale_grad.shape[1]), jnp.float32)

    for j in range(row_count):
        term = dot(low, weights[j][...], BOTH_LAST)

        @pl.when(at == 0)
        def _():
            total[j] = term

        @pl.when(at > 0)
        def _():
            total[j] = total[j] + term

    @pl.when(at == pl.num_programs(0) - 1)
    def _():
        for j in range(row_count):
            start = pl.multiple_of((me[1] ^ j) * rows, rows)
            grad_hidden[:, pl.ds(start, rows)] = total[j].astype(jnp.bfloat16)


def backward(me, params, mask, cotangent, preact, weights, parts):
    rows, width = preact.shape
    row_count = len(weights)
    cols = 512
    wide = pl.BlockSpec((rows, cols), lambda i, me: (0, i))
    narrow = pl.BlockSpec((STAT_ROWS, cols), lambda i, me: (0, i))

    def kernel(*refs):
        backward_kernel(*refs, row_count=row_count)

    return call(
        kernel,
        flops=2 * rows * width * width,
        nbytes=2 * width * width + 12 * rows * width,
        vmem_mb=40,
        grid_spec=pltpu.PrefetchScalarGridSpec(
            num_scalar_prefetch=1,
            grid=(width // cols,),
            in_specs=[
                pl.BlockSpec((3, cols), lambda i, me: (0, i)),
                pl.BlockSpec((rows, 1), lambda i, me: (0, 0)),
                wide,
                wide,
            ]
            + [pl.BlockSpec((w.shape[0], cols), lambda i, me: (0, i)) for w in weights]
            + [narrow] * len(parts),
            out_specs=[
                wide,
                wide,
                pl.BlockSpec((rows, width), lambda i, me: (0, 0)),
                narrow,
            ],
            scratch_shapes=[
                pltpu.VMEM((len(parts), STAT_ROWS, cols), jnp.float32),
                pltpu.VMEM((row_count, rows, rows), jnp.float32),
            ],
        ),
        out_shape=[
            jax.ShapeDtypeStruct((rows, width), jnp.bfloat16),
            jax.ShapeDtypeStruct((rows, width), jnp.bfloat16),
            jax.ShapeDtypeStruct((rows, width), jnp.bfloat16),
            jax.ShapeDtypeStruct((STAT_ROWS, width), jnp.float32),
        ],
        name="backward",
    )(me, params, mask, cotangent, preact, *weights, *parts)


def slots_kernel(flip, grads, *outs):
    side = outs[0].shape[0]
    total = dot(flip[side:, :], grads[...]).astype(jnp.bfloat16)
    for k, out in enumerate(outs):
        out[...] = total[k * side : (k + 1) * side]


def slots(flip, grads, side):
    rows, width = grads.shape
    count = flip.shape[0] // side - 1
    cols = 256
    return call(
        slots_kernel,
        flops=2 * flip.size * width,
        nbytes=2 * (flip.size + grads.size + count * side * width),
        vmem_mb=16 + (2 * flip.size * 2 + 6 * count * side * cols * 2 >> 20),
        grid=(width // cols,),
        in_specs=[
            pl.BlockSpec(flip.shape, lambda i: (0, 0)),
            pl.BlockSpec((rows, cols), lambda i: (0, i)),
        ],
        out_specs=[pl.BlockSpec((side, cols), lambda i: (0, i))] * count,
        out_shape=[jax.ShapeDtypeStruct((side, width), jnp.bfloat16)] * count,
        name="slots",
    )(flip, grads)


def outer_kernel(hidden_flip, grads, keep, send):
    half = keep.shape[0]
    low = dot(hidden_flip[...], grads[...]).astype(jnp.bfloat16)
    keep[...] = low[:half]
    send[...] = low[half:]


def outer(hidden_flip, grads, part, parts):
    width, rows = hidden_flip.shape
    span = width // parts
    cols = 256
    first = part * span // cols
    out = pl.BlockSpec((width // 2, cols), lambda i: (0, i))
    return call(
        outer_kernel,
        flops=2 * rows * width * span,
        nbytes=2 * (hidden_flip.size + rows * span + width * span),
        vmem_mb=24,
        grid=(span // cols,),
        in_specs=[
            pl.BlockSpec(hidden_flip.shape, lambda i: (0, 0)),
            pl.BlockSpec((rows, cols), lambda i: (0, i + first)),
        ],
        out_specs=[out, out],
        out_shape=[jax.ShapeDtypeStruct((width // 2, span), jnp.bfloat16)] * 2,
        name="outer",
    )(hidden_flip, grads)


def return_kernel(picks, flips_and_grads, returned, out, total):
    flips, grads = flips_and_grads
    blocks, side = total.shape[0], total.shape[1]
    result = dot(flips[0][...], grads[0][...])
    for flip, grad in zip(flips[1:], grads[1:]):
        result += dot(flip[...], grad[...])
    for b in range(blocks):
        total[b] = result[b * side : (b + 1) * side]
    for k, ref in enumerate(returned):
        b = picks[k]

        @pl.when(b >= 0)
        def _():
            total[b] = total[b] + ref[...].astype(jnp.float32)

    for b in range(blocks):
        out[b * side : (b + 1) * side, :] = total[b].astype(jnp.bfloat16)


def give_back(picks, flips, grads, returned):
    rows, width = grads[0].shape
    side = returned[0].shape[0]
    row_count = len(flips)
    cols = 256

    def kernel(picks, *refs):
        flip_refs, rest = refs[:row_count], refs[row_count:]
        return_kernel(
            picks, (flip_refs, rest[:row_count]), rest[row_count:-2], rest[-2], rest[-1]
        )

    return call(
        kernel,
        flops=2 * rows * rows * row_count * width,
        nbytes=2 * (row_count * (rows * rows + rows * width) + (len(returned) * side + rows) * width),
        vmem_mb=20 + (6 * len(returned) * side * cols * 2 >> 20),
        grid_spec=pltpu.PrefetchScalarGridSpec(
            num_scalar_prefetch=1,
            grid=(width // cols,),
            in_specs=[pl.BlockSpec((rows, rows), lambda i, p: (0, 0))] * row_count
            + [pl.BlockSpec((rows, cols), lambda i, p: (0, i))] * row_count
            + [pl.BlockSpec((side, cols), lambda i, p: (0, i))] * len(returned),
            out_specs=pl.BlockSpec((rows, cols), lambda i, p: (0, i)),
            scratch_shapes=[pltpu.VMEM((rows // side, side, cols), jnp.float32)],
        ),
        out_shape=jax.ShapeDtypeStruct((rows, width), jnp.bfloat16),
        name="give_back",
    )(picks, *flips, *grads, *returned)


def lamb_step(value, grad, first, second, decay):
    first_new = DECAY_FIRST * first + (1.0 - DECAY_FIRST) * grad
    second_new = DECAY_SECOND * second + (1.0 - DECAY_SECOND) * grad * grad
    update = (
        first_new
        / (1.0 - DECAY_FIRST**STEP)
        / (jnp.sqrt(second_new / (1.0 - DECAY_SECOND**STEP)) + ADAM_EPS)
        + decay * value
    )
    return (first_new, second_new, update)


def sum_all(value, dom_count, row_count):
    step = 1
    while step < row_count:
        value = value + swap(value, 0, step)
        step *= 2
    step = 1
    while step < dom_count:
        value = value + swap(value, step, 0)
        step *= 2
    return value


def reduce_weight(keep, send, dom_at, dom_count):
    half = keep.shape[0] // 2
    f32, bf = jnp.float32, jnp.bfloat16
    near = swap(send, 0, 1)
    cross = (keep[half:].astype(f32) + near[half:].astype(f32)).astype(bf)
    far = swap(cross, 0, 2)
    total = (keep[:half].astype(f32) + near[:half].astype(f32) + far.astype(f32)).astype(bf)
    step, rows = 1, half
    while step < dom_count:
        rows //= 2
        bit = (dom_at // step) % 2
        other = lax.dynamic_slice_in_dim(total, (1 - bit) * rows, rows, 0)
        mine = lax.dynamic_slice_in_dim(total, bit * rows, rows, 0)
        total = (mine.astype(f32) + swap(other, step, 0).astype(f32)).astype(bf)
        step *= 2
    return total


def collect_weight(total, dom_at, dom_count):
    step = dom_count // 2
    while step >= 1:
        bit = (dom_at // step) % 2
        other = swap(total, step, 0)
        total = jnp.where(
            bit == 0,
            jnp.concatenate([total, other], axis=0),
            jnp.concatenate([other, total], axis=0),
        )
        step //= 2
    return total


def on_device(
    features,
    adjacency,
    tile_values,
    tile_block,
    tile_slot,
    tile_count,
    send_block,
    node_mask,
    weight,
    params,
    weight_first,
    weight_second,
    params_first,
    params_second,
    cotangent,
):
    dom_count, row_count = lax.axis_size("dom"), lax.axis_size("row")
    dom_at, row_at = lax.axis_index("dom"), lax.axis_index("row")
    rows = features.shape[0]
    side = tile_values.shape[1]
    me = jnp.stack([dom_at, row_at]).astype(jnp.int32)
    sends = send_block[0]
    picks = jnp.stack([sends[dom_at ^ k] for k in range(1, dom_count)])
    mask = node_mask.astype(jnp.float32)[:, None]

    arrived = []
    for k in reversed(range(1, dom_count)):
        block = jnp.maximum(picks[k - 1], 0)
        arrived.append(
            swap(lax.dynamic_slice_in_dim(features, block * side, side, 0), k, 0)
        )
    arrived = arrived[::-1]
    near_features = spread_rows(features)
    near_weights = spread_rows(weight.astype(jnp.bfloat16))

    wide, flip, halo, halo_flip = prepare(
        me, tile_block, tile_slot, tile_count, adjacency, tile_values, dom_count
    )
    flips = [flip[:rows]] + [
        swap(flip[j * rows : (j + 1) * rows], 0, j) for j in range(1, row_count)
    ]
    hidden, hidden_flip = gather(me, wide, halo, near_features, arrived)
    preact, stats = linear(hidden, params, mask, cotangent, near_weights)
    stat_at, parts = exchange_stats(stats, dom_at, row_at, dom_count, row_count)
    me = jnp.concatenate([me, stat_at[None]])
    output, grad_pre, grad_hidden, sums = backward(
        me, params, mask, cotangent, preact, near_weights, parts
    )

    returned = [
        swap(piece, k + 1, 0) for k, piece in enumerate(slots(halo_flip, grad_hidden, side))
    ]
    near_grads = spread_rows(grad_hidden)

    pieces = []
    for part in range(WEIGHT_PARTS):
        keep, send = outer(hidden_flip, grad_pre, part, WEIGHT_PARTS)
        pieces.append(reduce_weight(keep, send, dom_at, dom_count))
    piece = jnp.concatenate(pieces, axis=1).astype(jnp.float32)
    piece_rows = piece.shape[0]
    start = 0
    step, span = 1, rows
    while step < dom_count:
        span //= 2
        start = start + ((dom_at // step) % 2) * span
        step *= 2
    cut = lambda v: lax.dynamic_slice_in_dim(v, start, piece_rows, 0)
    weight_piece = cut(weight)
    update_piece = lamb_step(
        weight_piece, piece, cut(weight_first), cut(weight_second), WEIGHT_DECAY
    )[2]
    squares = jnp.stack([jnp.sum(weight_piece * weight_piece), jnp.sum(update_piece * update_piece)])
    squares = sum_all(jnp.pad(squares[None], ((0, 7), (0, 126))), dom_count, row_count)
    weight_norms = jnp.sqrt(squares[0, :2])
    weight_grad = jnp.concatenate(
        [collect_weight(p, dom_at, dom_count) for p in pieces], axis=1
    ).astype(jnp.float32)
    weight_first_new, weight_second_new, weight_update = lamb_step(
        weight, weight_grad, weight_first, weight_second, WEIGHT_DECAY
    )
    weight_new = (
        weight - LEARN_RATE * (weight_norms[0] / (weight_norms[1] + TRUST_EPS)) * weight_update
    )

    grad_features = give_back(picks, flips, near_grads, returned)

    bias_grad = sum_all(sums, dom_count, row_count)[0:1]
    param_grads = jnp.concatenate([bias_grad, sums[1:3]], axis=0)
    params_first_new, params_second_new, param_update = lamb_step(
        params, param_grads, params_first, params_second, 0.0
    )
    param_norms = jnp.sqrt(jnp.sum(params * params, axis=1, keepdims=True))
    update_norms = jnp.sqrt(jnp.sum(param_update * param_update, axis=1, keepdims=True))
    params_new = params - LEARN_RATE * (param_norms / (update_norms + TRUST_EPS)) * param_update
    norms = jnp.concatenate(
        [weight_norms[None, :], jnp.concatenate([param_norms, update_norms], axis=1)], axis=0
    )
    return (
        output,
        grad_features,
        weight_new,
        weight_new.astype(jnp.bfloat16),
        weight_first_new,
        weight_second_new,
        params_new,
        params_first_new,
        params_second_new,
        norms,
    )


def solution(mesh):
    in_specs = (
        P(("dom", "row"), None),
        P(("dom", "row"), None),
        P(("dom", "row"), None, None),
        P(("dom", "row")),
        P(("dom", "row")),
        P(("dom", "row")),
        P(("dom", "row"), None),
        P(("dom", "row")),
        P("row", None),
        P(),
        P("row", None),
        P("row", None),
        P(),
        P(),
        P(("dom", "row"), None),
    )
    out_specs = (
        P(("dom", "row"), None),
        P(("dom", "row"), None),
        P("row", None),
        P("row", None),
        P("row", None),
        P("row", None),
        P(),
        P(),
        P(),
        P(),
    )
    return jax.shard_map(
        on_device, mesh=mesh, in_specs=in_specs, out_specs=out_specs, check_vma=False
    )
```

```python
import math

import jax
import jax.numpy as jnp
from jax import lax
from jax.experimental import pallas as pl
from jax.experimental.pallas import tpu as pltpu
from jax.sharding import PartitionSpec as P

STEP = 5


SELF_LOOP = 1.0
NORM_EPS = 1e-05
DECAY_FIRST = 0.5
DECAY_SECOND = 0.5
ADAM_EPS = 1e-06
WEIGHT_DECAY = 0.01
LEARN_RATE = 0.5
TRUST_EPS = 1e-06

AXES = ("dom", "row")
GELU_ROOT = math.sqrt(2.0 / math.pi)
GELU_CUBE = 0.044715
STAT_ROWS = 8
LANES = 128
COLS = 256
WHOLE_HALO = 2048
SLOT_GROUP = 7

ANY_ROWS = (((1,), (0,)), ((), ()))
BOTH_LAST = (((1,), (1,)), ((), ()))
SMEM = pl.BlockSpec(memory_space=pltpu.SMEM)
VMEM = pl.BlockSpec(memory_space=pltpu.VMEM)
ANY = pl.BlockSpec(memory_space=pl.ANY)
SDS = jax.ShapeDtypeStruct


def dot(left, right, dims=ANY_ROWS):
    return lax.dot_general(left, right, dims, preferred_element_type=jnp.float32)


def swap(value, dom_flip, row_flip):
    dom_count, row_count = lax.axis_size("dom"), lax.axis_size("row")
    pairs = [
        (d * row_count + r, (d ^ dom_flip) * row_count + (r ^ row_flip))
        for d in range(dom_count)
        for r in range(row_count)
    ]
    return lax.ppermute(value, AXES, pairs)


def hold(value, *others):
    return lax.optimization_barrier((value, *others))[0]


def call(kernel, *, flops, vmem_mb=56, **kw):
    return pl.pallas_call(
        kernel,
        cost_estimate=pl.CostEstimate(flops=int(flops), bytes_accessed=0, transcendentals=0),
        compiler_params=pltpu.CompilerParams(vmem_limit_bytes=vmem_mb << 20),
        **kw,
    )


def columns(width, blocked):
    if not blocked:
        return {}, lambda height: VMEM, lambda shape: VMEM
    grid = {"grid": (width // COLS,)}
    block = lambda height: pl.BlockSpec((height, COLS), lambda i: (0, i))
    whole = lambda shape: pl.BlockSpec(shape, lambda i: (0,) * len(shape))
    return grid, block, whole


def turns(dom_count):
    half = dom_count // 2
    far = sorted(range(half, dom_count), key=lambda k: (k % 2, k))
    near = sorted(range(1, half), key=lambda k: (k % 2 == 0, k))
    cut = lambda order, n, of: order[n * len(order) // of : (n + 1) * len(order) // of]
    return [cut(far, n, 4) for n in range(4)], [cut(near, n, 3) for n in range(3)]


def send_in_turn(piece, order, arrived, *first):
    for key in order:
        value = hold(piece(key), *first) if first else piece(key)
        arrived[key] = swap(value, key[0], 0)
        first = (arrived[key],)
    return first[0]


def prepare_kernel(
    me, sends, block_ref, slot_ref, count_ref, adj_ref, tile_ref, *refs
):
    wide, flip, halo, halo_flip, chooser, total = refs
    rows = adj_ref.shape[0]
    row_count = adj_ref.shape[1] // rows
    blocks, peers, side = total.shape[0], total.shape[1], total.shape[2]
    for j in range(row_count):
        start = pl.multiple_of((me[1] ^ j) * rows, rows)
        piece = adj_ref[:, pl.ds(start, rows)]
        if j == 0:
            at_row = lax.broadcasted_iota(jnp.int32, (rows, rows), 0)
            at_col = lax.broadcasted_iota(jnp.int32, (rows, rows), 1)
            wide_piece = piece.astype(jnp.float32)
            piece = jnp.where(at_row == at_col, (1.0 + SELF_LOOP) * wide_piece, wide_piece).astype(
                jnp.bfloat16
            )
        wide[:, j * rows : (j + 1) * rows] = piece
        flip[j * rows : (j + 1) * rows, :] = piece.T
    total[...] = jnp.zeros(total.shape, total.dtype)

    def add(t, carry):
        b = block_ref[t]
        k = slot_ref[t] ^ me[0]
        total[b, k] = total[b, k] + tile_ref[t].astype(jnp.float32)
        return carry

    lax.fori_loop(0, count_ref[0], add, 0)
    for b in range(blocks):
        for k in range(peers):
            piece = total[b, k].astype(jnp.bfloat16)
            halo[b * side : (b + 1) * side, k * side : (k + 1) * side] = piece
            halo_flip[k * side : (k + 1) * side, b * side : (b + 1) * side] = piece.T
    same = lax.broadcasted_iota(jnp.int32, (side, side), 0) == lax.broadcasted_iota(
        jnp.int32, (side, side), 1
    )
    for k in range(peers - 1):
        for b in range(blocks):
            chooser[b * side : (b + 1) * side, k * side : (k + 1) * side] = jnp.where(
                jnp.logical_and(same, sends[me[0] ^ (k + 1)] == b), 1.0, 0.0
            ).astype(jnp.bfloat16)


def prepare(me, sends, tile_block, tile_slot, tile_count, adjacency, tiles, peers):
    rows, part = adjacency.shape
    side = tiles.shape[1]
    bf = jnp.bfloat16
    return call(
        prepare_kernel,
        flops=tiles.size,
        vmem_mb=20 + (10 * rows * peers * side >> 20),
        in_specs=[SMEM] * 5 + [VMEM] * 2,
        out_specs=[VMEM] * 5,
        out_shape=[
            SDS((rows, part), bf),
            SDS((part, rows), bf),
            SDS((rows, peers * side), bf),
            SDS((peers * side, rows), bf),
            SDS((rows, (peers - 1) * side), bf),
        ],
        scratch_shapes=[pltpu.VMEM((rows // side, peers, side, side), jnp.float32)],
        name="prepare",
    )(me, sends, tile_block, tile_slot, tile_count, adjacency, tiles)


def outgoing_kernel(me, sends, source, *targets):
    halves, blocks = targets[:2], targets[2:]
    rows, side = halves[0].shape[0], blocks[0].shape[0]
    for n, target in enumerate(halves):
        target[...] = source[n * rows : (n + 1) * rows, :]
    for k, target in enumerate(blocks):
        block = jnp.maximum(sends[me[0] ^ (k + 1)], 0)
        target[...] = source[pl.ds(pl.multiple_of(block * side, side), side), :]


def outgoing(me, sends, features, side):
    rows, width = features.shape
    count = sends.shape[0] - 1
    low = features.dtype
    first, second, *blocks = call(
        outgoing_kernel,
        flops=0,
        vmem_mb=12 + (count * side * width >> 19),
        in_specs=[SMEM, SMEM, VMEM],
        out_specs=[VMEM] * (2 + count),
        out_shape=[SDS((rows // 2, width), low)] * 2 + [SDS((side, width), low)] * count,
        name="outgoing",
    )(me, sends, features)
    return first, second, blocks


def near_kernel(wide, *refs):
    sources, out = refs[:-1], refs[-1]
    for c in range(out.shape[1] // COLS):
        cs = slice(c * COLS, (c + 1) * COLS)
        total, done = 0.0, 0
        for ref in sources:
            total += dot(wide[:, done : done + ref.shape[0]], ref[:, cs])
            done += ref.shape[0]
        out[:, cs] = total


def near(wide, sources):
    rows, width = sources[0].shape
    return call(
        near_kernel,
        flops=2 * wide.size * width,
        vmem_mb=16,
        in_specs=[VMEM] * (1 + len(sources)),
        out_specs=VMEM,
        out_shape=SDS((rows, width), jnp.float32),
        name="near",
    )(wide, *sources)


def halo_kernel(me, base, halo, *refs, row_count, blocked):
    arrived, (hidden, hidden_flip) = refs[:-2], refs[-2:]
    rows, side = hidden.shape[0], arrived[0].shape[0]
    per = rows // COLS
    count = base.shape[1] // COLS
    for c in range(count):
        cs = slice(c * COLS, (c + 1) * COLS)
        at = c + (pl.program_id(0) * count if blocked else 0)
        pieces = jnp.concatenate([ref[:, cs] for ref in arrived], axis=0)
        low = (base[:, cs] + dot(halo[:, side:], pieces)).astype(jnp.bfloat16)
        hidden[:, pl.ds(pl.multiple_of(at * COLS, COLS), COLS)] = low
        j = (at // per) ^ me[1]
        start = pl.multiple_of(j // 2 * rows + at % per * COLS, COLS)
        hidden_flip[j % 2, pl.ds(start, COLS), :] = low.T


def add_halo(me, base, halo, arrived, row_count):
    rows, width = base.shape
    blocked = halo.shape[1] > WHOLE_HALO
    grid, block, whole = columns(width, blocked)

    def kernel(*refs):
        halo_kernel(*refs, row_count=row_count, blocked=blocked)

    return call(
        kernel,
        flops=2 * halo.size * width,
        vmem_mb=56 if blocked else 16,
        in_specs=[SMEM, block(rows), whole(halo.shape)]
        + [block(a.shape[0]) for a in arrived],
        out_specs=[whole((rows, width)), whole((2, width // 2, rows))],
        out_shape=[SDS((rows, width), jnp.bfloat16), SDS((2, width // 2, rows), jnp.bfloat16)],
        name="add_halo",
        **grid,
    )(me, base, halo, *arrived)


def gelu_parts(v):
    inner = GELU_ROOT * (v + GELU_CUBE * (v * v * v))
    return jnp.tanh(inner)


def weight_starts(me, rows):
    half = rows // 2
    starts = [me[1] * rows, (me[1] ^ 1) * rows]
    for j in (2, 3):
        starts += [(me[1] ^ j) * rows, (me[1] ^ j) * rows + half]
    return [pl.multiple_of(start, half) for start in starts]


def linear_kernel(me, hidden, params, mask_ref, cot_ref, *refs):
    weights, (pre_first, pre_second, stats, act_ref) = refs[:-4], refs[-4:]
    rows, width = hidden.shape
    starts = weight_starts(me, rows)
    mask = mask_ref[...]
    count = jnp.sum(mask[:, 0:1])
    stats[4:8, :] = jnp.full((4, width), count, jnp.float32)
    for c in range(width // COLS):
        cs = slice(c * COLS, (c + 1) * COLS)
        v = params[0:1, cs] + sum(
            dot(hidden[:, pl.ds(start, ref.shape[0])], ref[:, cs])
            for start, ref in zip(starts, weights)
        )
        span = width // 2
        preact = pre_second if c * COLS >= span else pre_first
        preact[:, c * COLS % span : c * COLS % span + COLS] = v
        act_ref[...] = 0.5 * v * (1.0 + gelu_parts(v))
        for part in range(COLS // LANES):
            here = slice(part * LANES, (part + 1) * LANES)
            there = slice(c * COLS + part * LANES, c * COLS + (part + 1) * LANES)
            act = act_ref[:, here]
            mean = jnp.sum(mask * act, axis=0, keepdims=True) / count
            centred = act - mean
            grad = mask * cot_ref[:, there].astype(jnp.float32)
            stats[0:1, there] = mean
            stats[1:2, there] = jnp.sum(mask * centred * centred, axis=0, keepdims=True)
            stats[2:3, there] = jnp.sum(grad, axis=0, keepdims=True)
            stats[3:4, there] = jnp.sum(grad * centred, axis=0, keepdims=True)


def linear(me, hidden, params, mask, cotangent, weights):
    rows, width = hidden.shape
    return call(
        linear_kernel,
        flops=2 * rows * width * width,
        vmem_mb=16,
        in_specs=[SMEM] + [VMEM] * (4 + len(weights)),
        out_specs=[VMEM] * 3,
        out_shape=[SDS((rows, width // 2), jnp.float32)] * 2
        + [SDS((STAT_ROWS, width), jnp.float32)],
        scratch_shapes=[pltpu.VMEM((rows, COLS), jnp.float32)],
        name="linear",
    )(me, hidden, params, mask, cotangent, *weights)


def merged(mine, refs, ordered):
    for i, ref in enumerate(refs):
        ordered[mine ^ i] = ref[...]
    parts = [ordered[i] for i in range(len(refs))]
    count = sum(p[4:5] for p in parts)
    mean = sum(p[4:5] * p[0:1] for p in parts) / count
    spread = sum(p[1:2] + p[4:5] * (p[0:1] - mean) * (p[0:1] - mean) for p in parts)
    shift = sum(p[2:3] for p in parts)
    scale = sum(p[3:4] + (p[0:1] - mean) * p[2:3] for p in parts)
    return mean, spread, shift, scale, count


def merge_kernel(mine, *refs):
    out, ordered = refs[-2:]
    for i, row in enumerate(merged(mine[0], refs[:-2], ordered)):
        out[i : i + 1, :] = row
    out[5:8, :] = jnp.zeros((3, out.shape[1]), jnp.float32)


def merge(mine, parts):
    return call(
        merge_kernel,
        flops=20 * parts[0].size * len(parts),
        vmem_mb=8,
        in_specs=[SMEM] + [VMEM] * len(parts),
        out_specs=VMEM,
        out_shape=SDS(parts[0].shape, jnp.float32),
        scratch_shapes=[pltpu.VMEM((len(parts),) + parts[0].shape, jnp.float32)],
        name="merge",
    )(mine[None], *parts)


def groups(dom_count, row_count):
    flips = [(0, 1 << i) for i in range(row_count.bit_length() - 1)]
    flips += [(1 << i, 0) for i in range(dom_count.bit_length() - 1)]
    return [flips[:1]] + [flips[i : i + 2] for i in range(1, len(flips), 2)]


def exchange(value, group):
    parts = [value]
    for i in range(1, 1 << len(group)):
        picked = [flip for j, flip in enumerate(group) if i >> j & 1]
        parts.append(swap(value, sum(f[0] for f in picked), sum(f[1] for f in picked)))
    return parts


def exchange_stats(stats, dom_at, row_at, dom_count, row_count):
    rounds = groups(dom_count, row_count)
    for n, group in enumerate(rounds):
        mine = jnp.int32(0)
        for i, (d, r) in enumerate(group):
            bit = (row_at & r) != 0 if r else (dom_at & d) != 0
            mine = mine + (bit.astype(jnp.int32) << i)
        parts = exchange(stats, group)
        if n < len(rounds) - 1:
            stats = merge(mine, parts)
    return mine, parts


def pair_sum(value, group, *others):
    parts = exchange(hold(value, *others) if others else value, group)
    while len(parts) > 1:
        parts = [a + b for a, b in zip(parts[::2], parts[1::2])]
    return parts[0]


def backward_kernel(mine, params, mask_ref, cot_in, pre_in, *refs, first, part_count):
    parts = refs[:part_count]
    grad_pre, sums, output, ordered, cot_ref, pre_ref, out_ref, sems, out_sems = refs[-9:]
    rows, span = grad_pre.shape
    step = rows // 4
    there = pl.ds(first, span)
    copies, sent = [], []
    for n in range(4):
        here = pl.ds(n * step, step)
        copies += [
            pltpu.make_async_copy(pre_in.at[here, :], pre_ref.at[here, :], sems.at[0, n]),
            pltpu.make_async_copy(cot_in.at[here, there], cot_ref.at[here, :], sems.at[1, n]),
        ]
    for copy in copies:
        copy.start()
    mean, spread, shift_grad, scale_sum, count = merged(mine[0], parts, ordered)
    inverse = lax.rsqrt(spread / count + NORM_EPS)
    scale_grad = scale_sum * inverse
    scale, shift = params[1:2, :], params[2:3, :]
    gain = scale * inverse
    shift_mean, scale_mean = shift_grad / count, scale_grad / count
    for i, row in enumerate((scale_grad, shift_grad)):
        sums[i + 1 : i + 2, :] = row[:, first : first + span]
    sums[3:8, :] = jnp.zeros((5, span), jnp.float32)
    for n in range(4):
        for copy in copies[2 * n : 2 * n + 2]:
            copy.wait()
        at = slice(n * step, (n + 1) * step)
        mask = mask_ref[at, :]
        for part in range(span // LANES):
            here = slice(part * LANES, (part + 1) * LANES)
            of = slice(first + part * LANES, first + (part + 1) * LANES)
            v = pre_ref[at, here]
            bend = gelu_parts(v)
            act = 0.5 * v * (1.0 + bend)
            normed = (act - mean[:, of]) * inverse[:, of]
            out_ref[at, here] = (mask * (scale[:, of] * normed + shift[:, of])).astype(jnp.bfloat16)
            grad_out = mask * cot_ref[at, here].astype(jnp.float32)
            grad_act = (
                mask * gain[:, of] * (grad_out - shift_mean[:, of] - normed * scale_mean[:, of])
            )
            slope = 0.5 * (1.0 + bend) + 0.5 * v * (1.0 - bend * bend) * (
                GELU_ROOT * (1.0 + 3.0 * GELU_CUBE * (v * v))
            )
            low = (grad_act * slope).astype(jnp.bfloat16)
            grad_pre[at, here] = low
            total = jnp.sum(low.astype(jnp.float32), axis=0, keepdims=True)
            sums[0:1, here] = total if n == 0 else sums[0:1, here] + total
        here = pl.ds(n * step, step)
        sent.append(
            pltpu.make_async_copy(out_ref.at[here, :], output.at[here, there], out_sems.at[n])
        )
        sent[-1].start()
    for copy in sent:
        copy.wait()


def backward(mine, params, mask, cotangent, preact, parts, part, output):
    rows, span = preact.shape
    width = cotangent.shape[1]
    before = [] if output is None else [output]

    def kernel(*refs):
        backward_kernel(*refs, first=part * span, part_count=len(parts))

    return call(
        kernel,
        flops=50 * rows * span,
        vmem_mb=56,
        in_specs=[SMEM, VMEM, VMEM, ANY, ANY] + [VMEM] * len(parts) + [ANY] * len(before),
        out_specs=[VMEM, VMEM, ANY],
        out_shape=[
            SDS((rows, span), jnp.bfloat16),
            SDS((STAT_ROWS, span), jnp.float32),
            SDS((rows, width), jnp.bfloat16),
        ],
        scratch_shapes=[
            pltpu.VMEM((len(parts), STAT_ROWS, width), jnp.float32),
            pltpu.VMEM((rows, span), jnp.bfloat16),
            pltpu.VMEM((rows, span), jnp.float32),
            pltpu.VMEM((rows, span), jnp.bfloat16),
            pltpu.SemaphoreType.DMA((2, 4)),
            pltpu.SemaphoreType.DMA((4,)),
        ],
        input_output_aliases={5 + len(parts): 2} if before else {},
        name="backward",
    )(mine[None], params, mask, cotangent, preact, *parts, *before)


def outers_kernel(me, *refs):
    inputs, outputs, buffers = list(refs[:6]), refs[6:10], refs[10:16]
    low_ref, sems, out_sems = refs[16:]
    inputs[0] = inputs[0].at[0]
    copies = [
        pltpu.make_async_copy(source, buffer, sems.at[n])
        for n, (source, buffer) in enumerate(zip(inputs, buffers))
    ]
    for copy in copies:
        copy.start()
    own_flip, near_flip = buffers[:2]
    rows, span = buffers[2].shape
    half = rows // 2
    sent = []
    for part in range(2):
        for n in ((0, 1, 2, 3), (4, 5))[part]:
            copies[n].wait()
        grad, near_grad = buffers[2 + 2 * part : 4 + 2 * part]
        for c in range(span // COLS):
            cs = slice(c * COLS, (c + 1) * COLS)
            total = dot(own_flip[...], grad[:, cs]) + dot(near_flip[...], near_grad[:, cs])
            low_ref[part, :, cs] = total.astype(jnp.bfloat16)
        for n in range(2):
            here = pl.ds(n * half, half)
            if part:
                kept, given = (
                    pl.multiple_of(n * rows + flag * half, half) for flag in (me[2], 1 - me[2])
                )
            else:
                kept, given = n * half, rows + n * half
            for m, start in enumerate((kept, given)):
                sent.append(
                    pltpu.make_async_copy(
                        low_ref.at[part, pl.ds(start, half), :],
                        outputs[2 * part + m].at[here, :],
                        out_sems.at[part, m, n],
                    )
                )
                sent[-1].start()
    for copy in sent:
        copy.wait()


def outers(me, hidden_flip, near_flip, grads, near_grads):
    rows, span = grads[0].shape
    low = jnp.bfloat16
    inputs = [hidden_flip, near_flip, grads[0], near_grads[0], grads[1], near_grads[1]]
    return call(
        outers_kernel,
        flops=0,
        vmem_mb=56,
        in_specs=[SMEM] + [ANY] * 6,
        out_specs=[ANY] * 4,
        out_shape=[SDS((rows, span), low)] * 4,
        scratch_shapes=[pltpu.VMEM(v.shape[-2:], low) for v in inputs]
        + [
            pltpu.VMEM((2, 2 * rows, span), low),
            pltpu.SemaphoreType.DMA((6,)),
            pltpu.SemaphoreType.DMA((2, 2, 2)),
        ],
        name="outers",
    )(me, *inputs)


def hidden_kernel(me, *refs, piece_total, slot_total, halved):
    inputs, refs = refs[: 3 + piece_total], refs[3 + piece_total :]
    outputs, refs = refs[: 1 + slot_total], refs[1 + slot_total :]
    buffers, refs = refs[: 3 + piece_total], refs[3 + piece_total :]
    grad_hidden, slots, sems, out_sem, slot_sems = refs
    grads, weights, halo_flip = buffers[:2], buffers[2:-1], buffers[-1]
    copies = [
        pltpu.make_async_copy(source, buffer, sems.at[n])
        for n, (source, buffer) in enumerate(zip(inputs, buffers))
    ]
    for copy in copies:
        copy.start()
    rows, width = grad_hidden.shape
    span = grads[0].shape[1]
    for copy in copies[:2]:
        copy.wait()
    for start, ref, copy in zip(weight_starts(me, rows), weights, copies[2:]):
        copy.wait()
        for c in range(ref.shape[0] // COLS):
            total = sum(
                dot(
                    grad[...],
                    ref[c * COLS : (c + 1) * COLS, p * span : (p + 1) * span],
                    BOTH_LAST,
                )
                for p, grad in enumerate(grads)
            )
            at = pl.multiple_of(start + c * COLS, COLS)
            grad_hidden[:, pl.ds(at, COLS)] = total.astype(jnp.bfloat16)
    out_copy = pltpu.make_async_copy(grad_hidden, outputs[0], out_sem)
    out_copy.start()
    copies[-1].wait()
    side = slots.shape[1] // SLOT_GROUP
    count = halo_flip.shape[0] // side - 1
    targets = list(outputs[1:])
    pending = {}
    for first in range(0, count, SLOT_GROUP):
        taken = min(SLOT_GROUP, count - first)
        buffer = first // SLOT_GROUP % 2
        for copy in pending.pop(buffer, ()):
            copy.wait()
        for c in range(width // COLS):
            cs = slice(c * COLS, (c + 1) * COLS)
            picked = halo_flip[(first + 1) * side : (first + 1 + taken) * side, :]
            slots[buffer, : taken * side, cs] = dot(picked, grad_hidden[:, cs]).astype(jnp.bfloat16)
        pending[buffer] = []
        for n in range(taken):
            for part in range(2 if first + n + 1 in halved else 1):
                target = targets.pop(0)
                height = target.shape[0]
                pending[buffer].append(
                    pltpu.make_async_copy(
                        slots.at[buffer, pl.ds(n * side + part * height, height), :],
                        target,
                        slot_sems.at[buffer, n, part],
                    )
                )
                pending[buffer][-1].start()
    for copy in sum(pending.values(), [out_copy]):
        copy.wait()


def hidden_grads(me, grads, weights, halo_flip, side, halved):
    rows, span = grads[0].shape
    width = 2 * span
    count = halo_flip.shape[0] // side - 1
    low = jnp.bfloat16
    shapes = []
    for k in range(1, count + 1):
        shapes += [SDS((side // 2, width), low)] * 2 if k in halved else [SDS((side, width), low)]
    inputs = [*grads, *weights, halo_flip]

    def kernel(*refs):
        hidden_kernel(*refs, piece_total=len(weights), slot_total=len(shapes), halved=halved)

    grad_hidden, *outs = call(
        kernel,
        flops=0,
        vmem_mb=56,
        in_specs=[SMEM] + [ANY] * len(inputs),
        out_specs=[ANY] * (1 + len(shapes)),
        out_shape=[SDS((rows, width), low)] + shapes,
        scratch_shapes=[pltpu.VMEM(v.shape, low) for v in inputs]
        + [
            pltpu.VMEM((rows, width), low),
            pltpu.VMEM((2 if count > SLOT_GROUP else 1, SLOT_GROUP * side, width), low),
            pltpu.SemaphoreType.DMA((len(inputs),)),
            pltpu.SemaphoreType.DMA,
            pltpu.SemaphoreType.DMA((2, SLOT_GROUP, 2)),
        ],
        name="hidden_grads",
    )(me, *inputs)
    slots = {}
    for k in range(1, count + 1):
        for part in range(2 if k in halved else 1):
            slots[k, part] = outs.pop(0)
    return grad_hidden, slots


def near_back_kernel(*refs, row_count):
    flips, grads, out = refs[:row_count], refs[row_count:-1], refs[-1]
    rows = flips[0].shape[0]
    for c in range(out.shape[1] // COLS):
        cs = slice(c * COLS, (c + 1) * COLS)
        total, done = 0.0, 0
        for grad in grads:
            depth = grad.shape[0]
            total += dot(flips[done // rows][:, done % rows : done % rows + depth], grad[:, cs])
            done += depth
        out[:, cs] = total


def near_back(flips, grads):
    rows, width = grads[0].shape

    def kernel(*refs):
        near_back_kernel(*refs, row_count=len(flips))

    return call(
        kernel,
        flops=2 * rows * rows * len(flips) * width,
        vmem_mb=56,
        in_specs=[VMEM] * (len(flips) + len(grads)),
        out_specs=VMEM,
        out_shape=SDS((rows, width), jnp.float32),
        name="near_back",
    )(*flips, *grads)


def return_kernel(chooser, base, *refs):
    returned, out = refs[:-1], refs[-1]
    for c in range(out.shape[1] // COLS):
        cs = slice(c * COLS, (c + 1) * COLS)
        pieces = jnp.concatenate([ref[:, cs] for ref in returned], axis=0)
        out[:, cs] = (base[:, cs] + dot(chooser[...], pieces)).astype(jnp.bfloat16)


def give_back(chooser, base, returned):
    rows, width = base.shape
    blocked = chooser.shape[1] > WHOLE_HALO
    grid, block, whole = columns(width, blocked)
    return call(
        return_kernel,
        flops=2 * rows * chooser.shape[1] * width,
        vmem_mb=56,
        in_specs=[whole(chooser.shape), block(rows)]
        + [block(r.shape[0]) for r in returned],
        out_specs=block(rows),
        out_shape=SDS((rows, width), jnp.bfloat16),
        name="give_back",
        **grid,
    )(chooser, base, *returned)


def lamb_step(value, grad, first, second, decay):
    first_new = DECAY_FIRST * first + (1.0 - DECAY_FIRST) * grad
    second_new = DECAY_SECOND * second + (1.0 - DECAY_SECOND) * grad * grad
    update = (
        first_new
        / (1.0 - DECAY_FIRST**STEP)
        / (jnp.sqrt(second_new / (1.0 - DECAY_SECOND**STEP)) + ADAM_EPS)
        + decay * value
    )
    return (first_new, second_new, update)


def first_sums_kernel(me, keep_a, came_a, keep_b, came_b, kept_a, sent_a, kept_b, sent_b):
    half = kept_a.shape[0]
    for flag, out in ((me[2], kept_a), (1 - me[2], sent_a)):
        rows = pl.ds(pl.multiple_of(flag * half, half), half)
        out[...] = (keep_a[rows, :].astype(jnp.float32) + came_a[rows, :].astype(jnp.float32)).astype(out.dtype)
    for n, out in enumerate((kept_b, sent_b)):
        rows = slice(n * half, (n + 1) * half)
        out[...] = (keep_b[rows, :].astype(jnp.float32) + came_b[rows, :].astype(jnp.float32)).astype(out.dtype)


def first_sums(me, keep_a, came_a, keep_b, came_b):
    rows, span = keep_a.shape
    kept, sent = SDS((rows // 2, span), jnp.float32), SDS((rows // 2, span), jnp.bfloat16)
    return call(
        first_sums_kernel,
        flops=0,
        vmem_mb=56,
        in_specs=[SMEM] + [VMEM] * 4,
        out_specs=[VMEM] * 4,
        out_shape=[kept, sent, kept, sent],
        name="first_sums",
    )(me, keep_a, came_a, keep_b, came_b)


def joined_kernel(flag, kept_a, came_a, kept_b, came_b, kept, sent):
    half, span = kept.shape[0], kept_a.shape[1]
    for n, (keep, came) in enumerate(((kept_a, came_a), (kept_b, came_b))):
        cs = slice(n * span, (n + 1) * span)
        for bit, out in ((flag[0], kept), (1 - flag[0], sent)):
            rows = pl.ds(pl.multiple_of(bit * half, half), half)
            out[:, cs] = (keep[rows, :] + came[rows, :].astype(jnp.float32)).astype(out.dtype)


def joined(flag, kept_a, came_a, kept_b, came_b):
    rows, span = kept_a.shape
    return call(
        joined_kernel,
        flops=0,
        vmem_mb=56,
        in_specs=[SMEM] + [VMEM] * 4,
        out_specs=[VMEM] * 2,
        out_shape=[
            SDS((rows // 2, 2 * span), jnp.float32),
            SDS((rows // 2, 2 * span), jnp.bfloat16),
        ],
        name="joined",
    )(flag[None], kept_a, came_a, kept_b, came_b)


def halved_kernel(flag, keep, came, kept, sent):
    half = kept.shape[0]
    for bit, out in ((flag[0], kept), (1 - flag[0], sent)):
        rows = pl.ds(pl.multiple_of(bit * half, half), half)
        out[...] = (keep[rows, :] + came[rows, :].astype(jnp.float32)).astype(out.dtype)


def halved_sums(flag, keep, came):
    rows, width = keep.shape
    return call(
        halved_kernel,
        flops=0,
        vmem_mb=56,
        in_specs=[SMEM] + [VMEM] * 2,
        out_specs=[VMEM] * 2,
        out_shape=[SDS((rows // 2, width), jnp.float32), SDS((rows // 2, width), jnp.bfloat16)],
        name="halved_sums",
    )(flag[None], keep, came)


def piece_kernel(start, kept, came, sums, value_in, first_in, second_in, piece, totals, value, first, second, sems):
    rows = piece.shape[0]
    here = pl.ds(pl.multiple_of(start[0], rows), rows)
    copies = [
        pltpu.make_async_copy(source.at[here, :], target, sems.at[n])
        for n, (source, target) in enumerate(
            zip((value_in, first_in, second_in), (value, first, second))
        )
    ]
    for copy in copies:
        copy.start()
    low = (kept[...] + came[...].astype(jnp.float32)).astype(jnp.bfloat16)
    piece[...] = low
    for copy in copies:
        copy.wait()
    update = lamb_step(
        value[...], low.astype(jnp.float32), first[...], second[...], WEIGHT_DECAY
    )[2]
    totals[0:1, :] = sums[0:1, :]
    totals[1:2, :] = jnp.sum(value[...] * value[...], axis=0, keepdims=True)
    totals[2:3, :] = jnp.sum(update * update, axis=0, keepdims=True)
    totals[3:8, :] = jnp.zeros((5, totals.shape[1]), jnp.float32)


def piece_totals(start, kept, came, sums, weight, first, second):
    rows, width = kept.shape
    return call(
        piece_kernel,
        flops=0,
        vmem_mb=56,
        in_specs=[SMEM, VMEM, VMEM, VMEM, ANY, ANY, ANY],
        out_specs=[VMEM, VMEM],
        out_shape=[SDS((rows, width), jnp.bfloat16), SDS((STAT_ROWS, width), jnp.float32)],
        scratch_shapes=[pltpu.VMEM((rows, width), jnp.float32)] * 3
        + [pltpu.SemaphoreType.DMA((3,))],
        name="piece_totals",
    )(start[None], kept, came, sums, weight, first, second)


def by_bit(flag, own, came):
    rows, width = own.shape
    mine = (jnp.arange(2, dtype=jnp.int32) == flag)[:, None, None]
    return jnp.where(mine, own[None], came[None]).reshape(2 * rows, width)


def on_device(
    features,
    adjacency,
    tile_values,
    tile_block,
    tile_slot,
    tile_count,
    send_block,
    node_mask,
    weight,
    params,
    weight_first,
    weight_second,
    params_first,
    params_second,
    cotangent,
):
    dom_count, row_count = lax.axis_size("dom"), lax.axis_size("row")
    dom_at, row_at = lax.axis_index("dom"), lax.axis_index("row")
    rows, width = features.shape
    side = tile_values.shape[1]
    side_bit = dom_at % 2
    me = jnp.stack([dom_at, row_at, side_bit]).astype(jnp.int32)
    sends = send_block[0]
    mask = jnp.broadcast_to(node_mask.astype(jnp.float32)[:, None], (rows, LANES))

    half = rows // 2
    low_weight = weight.astype(jnp.bfloat16)
    first_half, second_half, blocks = outgoing(me, sends, features, side)
    wide, flip, halo, halo_flip, chooser = prepare(
        me, sends, tile_block, tile_slot, tile_count, adjacency, tile_values, dom_count
    )

    far, light = turns(dom_count)
    arrived = {}
    whole = lambda order: [(k, 0) for k in order]
    out = lambda key: blocks[key[0] - 1]
    far_first = swap(first_half, 0, 2)
    near_features = swap(features, 0, 1)
    turn = [
        far_first,
        near_features,
        send_in_turn(out, whole(far[0]), arrived),
        send_in_turn(out, whole(light[0]), arrived),
    ]
    far_second = swap(hold(second_half, *turn), 0, 2)
    cross = [swap(hold(far_first, *turn), 0, 1)]
    turn = [
        far_second,
        cross[0],
        send_in_turn(out, whole(far[1]), arrived, *turn),
        send_in_turn(out, whole(light[1]), arrived, *turn),
    ]
    over_y = swap(hold(low_weight[:half], *turn), 0, 2)
    cross.append(swap(hold(far_second, *turn), 0, 1))
    near_weight = swap(hold(low_weight, *turn), 0, 1)
    turn = [
        over_y,
        cross[1],
        near_weight,
        send_in_turn(out, whole(far[2]), arrived, *turn),
        send_in_turn(out, whole(light[2]), arrived, *turn),
    ]
    over_y_too = swap(hold(low_weight[half:], *turn), 0, 2)
    send_in_turn(out, whole(far[3]), arrived, *turn)
    base = near(wide, [features, near_features, far_first, far_second] + cross)
    weights = [
        low_weight,
        near_weight,
        over_y,
        over_y_too,
        swap(hold(over_y, base), 0, 1),
        swap(over_y_too, 0, 1),
    ]
    arrived = [arrived[k, 0] for k in range(1, dom_count)]
    hidden, hidden_flip = add_halo(me, base, halo, arrived, row_count)
    pre_first, pre_second, stats = linear(me, hidden, params, mask, cotangent, weights)
    mine, parts = exchange_stats(stats, dom_at, row_at, dom_count, row_count)
    near_flip = swap(hidden_flip[1], 0, 1)

    mine = hold(mine, near_flip)
    output, grads, near_pre, sums = None, [], [], []
    for part, preact in enumerate((pre_first, pre_second)):
        grad_pre, sum_part, output = backward(
            mine, params, mask, cotangent, preact, parts, part, output
        )
        grads.append(grad_pre)
        near_pre.append(swap(grad_pre, 0, 1))
        sums.append(sum_part)
    sums = jnp.concatenate(sums, axis=1)
    halved = far[2] + far[3]
    keep_a, send_a, keep_b, send_b = outers(me, hidden_flip, near_flip, grads, near_pre)
    grad_hidden, slots = hidden_grads(me, grads, weights, halo_flip, side, halved)

    returned = {}
    part_of = lambda order, n: [(k, n) for k in order]
    bit = lambda step: (dom_at // step) % 2
    blocks_back = lambda order, *turn: send_in_turn(lambda k: slots[k], order, returned, *turn)

    turn_flip = lambda j, *turn: swap(hold(flip[j * rows : (j + 1) * rows], *turn), 0, j)
    rounds = groups(dom_count, row_count)

    start, span = 0, rows
    for step in [1 << n for n in range(dom_count.bit_length() - 1)]:
        span //= 2
        start = start + bit(step) * span
    small_steps = sum(rounds, [])

    flips = [flip[:rows], turn_flip(1, send_a), None, None]
    turn = [swap(send_a, 0, 2), swap(send_b, 1, 0), flips[1], grad_hidden]
    kept_a, sent_a, kept_b, sent_b = first_sums(me, keep_a, turn[0], keep_b, turn[1])
    near_grad = swap(hold(grad_hidden, *turn), 0, 1)
    flips[2] = turn_flip(2, *turn)
    turn = [
        swap(hold(sent_a, *turn), 1, 0),
        swap(hold(sent_b, *turn), 0, 2),
        blocks_back(whole(far[0]), *turn),
        near_grad,
        flips[2],
    ]
    kept, sent = joined(bit(2), kept_a, turn[0], kept_b, turn[1])
    steps = [1 << n for n in range(1, dom_count.bit_length() - 1)]
    quarter = rows // 4
    grad_parts, cross = [], []

    def over_y_back(*turn):
        n = len(grad_parts)
        grad_parts.append(
            swap(hold(grad_hidden[n * quarter : (n + 1) * quarter], *turn), 0, 2)
        )
        if n:
            cross.append(swap(hold(grad_parts[n - 1], *turn), 0, 1))
        return [grad_parts[n]] + cross[n - 1 : n]

    beside = [
        [part_of(far[2], 0), whole(light[0])],
        [part_of(far[2], 1), whole(light[1])],
        [part_of(far[3], 0)],
        [part_of(far[3], 1)],
    ]
    for n, step in enumerate(steps):
        came = swap(hold(sent, *turn), step, 0)
        more = []
        if n < 2:
            more = [blocks_back(order, *turn) for order in beside[n]] + over_y_back(*turn)
        turn = [came] + more
        if step < dom_count // 2:
            kept, sent = halved_sums(bit(2 * step), kept, came)
    weight_grad, totals = piece_totals(
        start, kept, came, sums, weight, weight_first, weight_second
    )
    for n, step in enumerate(reversed(steps)):
        came = swap(hold(weight_grad, *turn), step, 0)
        more = []
        if n < 2:
            more = [blocks_back(order, *turn) for order in beside[2 + n]] + over_y_back(*turn)
            for flip_bits in small_steps[:3] if n == 0 else small_steps[3:]:
                totals = pair_sum(totals, [flip_bits], *turn)
            more.append(totals)
        weight_grad = by_bit(bit(step), weight_grad, came)
        turn = [came] + more
    came = swap(hold(weight_grad, *turn), 1, 0)
    blocks_back(whole(far[1]), *turn)
    blocks_back(whole(light[2]), *turn)
    cross.append(swap(hold(grad_parts[-1], *turn), 0, 1))
    flips[3] = turn_flip(3, *turn)
    bias_grad = totals[0:1]
    weight_norms = jnp.sqrt(jnp.sum(totals[1:3], axis=1))
    base = near_back(flips, [grad_hidden, near_grad] + grad_parts + cross)
    weight_grad = by_bit(bit(1), weight_grad, hold(came, base)).astype(jnp.float32)
    returned = [returned[key] for key in sorted(returned)]
    weight_first_new, weight_second_new, weight_update = lamb_step(
        weight, weight_grad, weight_first, weight_second, WEIGHT_DECAY
    )
    weight_new = (
        weight - LEARN_RATE * (weight_norms[0] / (weight_norms[1] + TRUST_EPS)) * weight_update
    )

    grad_features = give_back(chooser, hold(base, weight_new), returned)
    param_grads = jnp.concatenate([bias_grad, sums[1:3]], axis=0)
    params_first_new, params_second_new, param_update = lamb_step(
        params, param_grads, params_first, params_second, 0.0
    )
    param_norms = jnp.sqrt(jnp.sum(params * params, axis=1, keepdims=True))
    update_norms = jnp.sqrt(jnp.sum(param_update * param_update, axis=1, keepdims=True))
    params_new = params - LEARN_RATE * (param_norms / (update_norms + TRUST_EPS)) * param_update
    norms = jnp.concatenate(
        [weight_norms[None, :], jnp.concatenate([param_norms, update_norms], axis=1)], axis=0
    )
    return (
        output,
        grad_features,
        weight_new,
        weight_new.astype(jnp.bfloat16),
        weight_first_new,
        weight_second_new,
        params_new,
        params_first_new,
        params_second_new,
        norms,
    )


def solution(mesh):
    in_specs = (
        P(("dom", "row"), None),
        P(("dom", "row"), None),
        P(("dom", "row"), None, None),
        P(("dom", "row")),
        P(("dom", "row")),
        P(("dom", "row")),
        P(("dom", "row"), None),
        P(("dom", "row")),
        P("row", None),
        P(),
        P("row", None),
        P("row", None),
        P(),
        P(),
        P(("dom", "row"), None),
    )
    out_specs = (
        P(("dom", "row"), None),
        P(("dom", "row"), None),
        P("row", None),
        P("row", None),
        P("row", None),
        P("row", None),
        P(),
        P(),
        P(),
        P(),
    )
    return jax.shard_map(
        on_device, mesh=mesh, in_specs=in_specs, out_specs=out_specs, check_vma=False
    )
```

```python
import math

import jax
import jax.numpy as jnp
from jax import lax
from jax.experimental import pallas as pl
from jax.experimental.pallas import tpu as pltpu
from jax.sharding import PartitionSpec as P

STEP = 5


SELF_LOOP = 1.0
NORM_EPS = 1e-05
DECAY_FIRST = 0.5
DECAY_SECOND = 0.5
ADAM_EPS = 1e-06
WEIGHT_DECAY = 0.01
LEARN_RATE = 0.5
TRUST_EPS = 1e-06

AXES = ("dom", "row")
GELU_ROOT = math.sqrt(2.0 / math.pi)
GELU_CUBE = 0.044715
STAT_ROWS = 8
LANES = 128
COLS = 256
WHOLE_HALO = 2048
SLOT_GROUP = 7

ANY_ROWS = (((1,), (0,)), ((), ()))
BOTH_LAST = (((1,), (1,)), ((), ()))
SMEM = pl.BlockSpec(memory_space=pltpu.SMEM)
VMEM = pl.BlockSpec(memory_space=pltpu.VMEM)
ANY = pl.BlockSpec(memory_space=pl.ANY)
SDS = jax.ShapeDtypeStruct


def dot(left, right, dims=ANY_ROWS):
    return lax.dot_general(left, right, dims, preferred_element_type=jnp.float32)


def swap(value, dom_flip, row_flip):
    dom_count, row_count = lax.axis_size("dom"), lax.axis_size("row")
    pairs = [
        (d * row_count + r, (d ^ dom_flip) * row_count + (r ^ row_flip))
        for d in range(dom_count)
        for r in range(row_count)
    ]
    return lax.ppermute(value, AXES, pairs)


def hold(value, *others):
    return lax.optimization_barrier((value, *others))[0]


def call(kernel, *, flops, vmem_mb=56, **kw):
    return pl.pallas_call(
        kernel,
        cost_estimate=pl.CostEstimate(flops=int(flops), bytes_accessed=0, transcendentals=0),
        compiler_params=pltpu.CompilerParams(vmem_limit_bytes=vmem_mb << 20),
        **kw,
    )


def columns(width, blocked):
    if not blocked:
        return {}, lambda height: VMEM, lambda shape: VMEM
    grid = {"grid": (width // COLS,)}
    block = lambda height: pl.BlockSpec((height, COLS), lambda i: (0, i))
    whole = lambda shape: pl.BlockSpec(shape, lambda i: (0,) * len(shape))
    return grid, block, whole


def turns(dom_count):
    half = dom_count // 2
    far = sorted(range(half, dom_count), key=lambda k: (k % 2, k))
    near = sorted(range(1, half), key=lambda k: (k % 2 == 0, k))
    cut = lambda order, n, of: order[n * len(order) // of : (n + 1) * len(order) // of]
    return [cut(far, n, 4) for n in range(4)], [cut(near, n, 3) for n in range(3)]


def send_in_turn(piece, order, arrived, *first):
    for key in order:
        value = hold(piece(key), *first) if first else piece(key)
        arrived[key] = swap(value, key[0], 0)
        first = (arrived[key],)
    return first[0]


def prepare_kernel(
    me, sends, block_ref, slot_ref, count_ref, adj_ref, tile_ref, *refs
):
    wide, flip, halo, halo_flip, chooser, total = refs
    rows = adj_ref.shape[0]
    row_count = adj_ref.shape[1] // rows
    blocks, peers, side = total.shape[0], total.shape[1], total.shape[2]
    for j in range(row_count):
        start = pl.multiple_of((me[1] ^ j) * rows, rows)
        piece = adj_ref[:, pl.ds(start, rows)]
        if j == 0:
            at_row = lax.broadcasted_iota(jnp.int32, (rows, rows), 0)
            at_col = lax.broadcasted_iota(jnp.int32, (rows, rows), 1)
            wide_piece = piece.astype(jnp.float32)
            piece = jnp.where(at_row == at_col, (1.0 + SELF_LOOP) * wide_piece, wide_piece).astype(
                jnp.bfloat16
            )
        wide[:, j * rows : (j + 1) * rows] = piece
        flip[j * rows : (j + 1) * rows, :] = piece.T
    total[...] = jnp.zeros(total.shape, total.dtype)

    def add(t, carry):
        b = block_ref[t]
        k = slot_ref[t] ^ me[0]
        total[b, k] = total[b, k] + tile_ref[t].astype(jnp.float32)
        return carry

    lax.fori_loop(0, count_ref[0], add, 0)
    for b in range(blocks):
        for k in range(peers):
            piece = total[b, k].astype(jnp.bfloat16)
            halo[b * side : (b + 1) * side, k * side : (k + 1) * side] = piece
            halo_flip[k * side : (k + 1) * side, b * side : (b + 1) * side] = piece.T
    same = lax.broadcasted_iota(jnp.int32, (side, side), 0) == lax.broadcasted_iota(
        jnp.int32, (side, side), 1
    )
    for k in range(peers - 1):
        for b in range(blocks):
            chooser[b * side : (b + 1) * side, k * side : (k + 1) * side] = jnp.where(
                jnp.logical_and(same, sends[me[0] ^ (k + 1)] == b), 1.0, 0.0
            ).astype(jnp.bfloat16)


def prepare(me, sends, tile_block, tile_slot, tile_count, adjacency, tiles, peers):
    rows, part = adjacency.shape
    side = tiles.shape[1]
    bf = jnp.bfloat16
    return call(
        prepare_kernel,
        flops=tiles.size,
        vmem_mb=20 + (10 * rows * peers * side >> 20),
        in_specs=[SMEM] * 5 + [VMEM] * 2,
        out_specs=[VMEM] * 5,
        out_shape=[
            SDS((rows, part), bf),
            SDS((part, rows), bf),
            SDS((rows, peers * side), bf),
            SDS((peers * side, rows), bf),
            SDS((rows, (peers - 1) * side), bf),
        ],
        scratch_shapes=[pltpu.VMEM((rows // side, peers, side, side), jnp.float32)],
        name="prepare",
    )(me, sends, tile_block, tile_slot, tile_count, adjacency, tiles)


def outgoing_kernel(me, sends, source, *targets):
    halves, blocks = targets[:2], targets[2:]
    rows, side = halves[0].shape[0], blocks[0].shape[0]
    for n, target in enumerate(halves):
        target[...] = source[n * rows : (n + 1) * rows, :]
    for k, target in enumerate(blocks):
        block = jnp.maximum(sends[me[0] ^ (k + 1)], 0)
        target[...] = source[pl.ds(pl.multiple_of(block * side, side), side), :]


def outgoing(me, sends, features, side):
    rows, width = features.shape
    count = sends.shape[0] - 1
    low = features.dtype
    first, second, *blocks = call(
        outgoing_kernel,
        flops=0,
        vmem_mb=12 + (count * side * width >> 19),
        in_specs=[SMEM, SMEM, VMEM],
        out_specs=[VMEM] * (2 + count),
        out_shape=[SDS((rows // 2, width), low)] * 2 + [SDS((side, width), low)] * count,
        name="outgoing",
    )(me, sends, features)
    return first, second, blocks


def near_kernel(wide, *refs):
    sources, out = refs[:-1], refs[-1]
    for c in range(out.shape[1] // COLS):
        cs = slice(c * COLS, (c + 1) * COLS)
        total, done = 0.0, 0
        for ref in sources:
            total += dot(wide[:, done : done + ref.shape[0]], ref[:, cs])
            done += ref.shape[0]
        out[:, cs] = total


def near(wide, sources):
    rows, width = sources[0].shape
    return call(
        near_kernel,
        flops=2 * wide.size * width,
        vmem_mb=16,
        in_specs=[VMEM] * (1 + len(sources)),
        out_specs=VMEM,
        out_shape=SDS((rows, width), jnp.float32),
        name="near",
    )(wide, *sources)


def halo_kernel(me, base, halo, *refs, row_count, blocked):
    arrived, (hidden, hidden_flip) = refs[:-2], refs[-2:]
    rows, side = hidden.shape[0], arrived[0].shape[0]
    per = rows // COLS
    count = base.shape[1] // COLS
    for c in range(count):
        cs = slice(c * COLS, (c + 1) * COLS)
        at = c + (pl.program_id(0) * count if blocked else 0)
        pieces = jnp.concatenate([ref[:, cs] for ref in arrived], axis=0)
        low = (base[:, cs] + dot(halo[:, side:], pieces)).astype(jnp.bfloat16)
        hidden[:, pl.ds(pl.multiple_of(at * COLS, COLS), COLS)] = low
        j = (at // per) ^ me[1]
        start = pl.multiple_of(j // 2 * rows + at % per * COLS, COLS)
        hidden_flip[j % 2, pl.ds(start, COLS), :] = low.T


def add_halo(me, base, halo, arrived, row_count):
    rows, width = base.shape
    blocked = halo.shape[1] > WHOLE_HALO
    grid, block, whole = columns(width, blocked)

    def kernel(*refs):
        halo_kernel(*refs, row_count=row_count, blocked=blocked)

    return call(
        kernel,
        flops=2 * halo.size * width,
        vmem_mb=56 if blocked else 16,
        in_specs=[SMEM, block(rows), whole(halo.shape)]
        + [block(a.shape[0]) for a in arrived],
        out_specs=[whole((rows, width)), whole((2, width // 2, rows))],
        out_shape=[SDS((rows, width), jnp.bfloat16), SDS((2, width // 2, rows), jnp.bfloat16)],
        name="add_halo",
        **grid,
    )(me, base, halo, *arrived)


def gelu_parts(v):
    inner = GELU_ROOT * (v + GELU_CUBE * (v * v * v))
    return jnp.tanh(inner)


def weight_starts(me, rows):
    half = rows // 2
    starts = [me[1] * rows, (me[1] ^ 1) * rows]
    for j in (2, 3):
        starts += [(me[1] ^ j) * rows, (me[1] ^ j) * rows + half]
    return [pl.multiple_of(start, half) for start in starts]


def linear_kernel(me, hidden, params, mask_ref, cot_ref, *refs):
    weights, (pre_first, pre_second, stats, act_ref) = refs[:-4], refs[-4:]
    rows, width = hidden.shape
    starts = weight_starts(me, rows)
    mask = mask_ref[...]
    count = jnp.sum(mask[:, 0:1])
    stats[4:8, :] = jnp.full((4, width), count, jnp.float32)
    for c in range(width // COLS):
        cs = slice(c * COLS, (c + 1) * COLS)
        v = params[0:1, cs] + sum(
            dot(hidden[:, pl.ds(start, ref.shape[0])], ref[:, cs])
            for start, ref in zip(starts, weights)
        )
        span = width // 2
        preact = pre_second if c * COLS >= span else pre_first
        preact[:, c * COLS % span : c * COLS % span + COLS] = v
        act_ref[...] = 0.5 * v * (1.0 + gelu_parts(v))
        for part in range(COLS // LANES):
            here = slice(part * LANES, (part + 1) * LANES)
            there = slice(c * COLS + part * LANES, c * COLS + (part + 1) * LANES)
            act = act_ref[:, here]
            mean = jnp.sum(mask * act, axis=0, keepdims=True) / count
            centred = act - mean
            grad = mask * cot_ref[:, there].astype(jnp.float32)
            stats[0:1, there] = mean
            stats[1:2, there] = jnp.sum(mask * centred * centred, axis=0, keepdims=True)
            stats[2:3, there] = jnp.sum(grad, axis=0, keepdims=True)
            stats[3:4, there] = jnp.sum(grad * centred, axis=0, keepdims=True)


def linear(me, hidden, params, mask, cotangent, weights):
    rows, width = hidden.shape
    return call(
        linear_kernel,
        flops=2 * rows * width * width,
        vmem_mb=16,
        in_specs=[SMEM] + [VMEM] * (4 + len(weights)),
        out_specs=[VMEM] * 3,
        out_shape=[SDS((rows, width // 2), jnp.float32)] * 2
        + [SDS((STAT_ROWS, width), jnp.float32)],
        scratch_shapes=[pltpu.VMEM((rows, COLS), jnp.float32)],
        name="linear",
    )(me, hidden, params, mask, cotangent, *weights)


def merged(mine, refs, ordered):
    for i, ref in enumerate(refs):
        ordered[mine ^ i] = ref[...]
    parts = [ordered[i] for i in range(len(refs))]
    count = sum(p[4:5] for p in parts)
    mean = sum(p[4:5] * p[0:1] for p in parts) / count
    spread = sum(p[1:2] + p[4:5] * (p[0:1] - mean) * (p[0:1] - mean) for p in parts)
    shift = sum(p[2:3] for p in parts)
    scale = sum(p[3:4] + (p[0:1] - mean) * p[2:3] for p in parts)
    return mean, spread, shift, scale, count


def merge_kernel(mine, *refs):
    out, ordered = refs[-2:]
    for i, row in enumerate(merged(mine[0], refs[:-2], ordered)):
        out[i : i + 1, :] = row
    out[5:8, :] = jnp.zeros((3, out.shape[1]), jnp.float32)


def merge(mine, parts):
    return call(
        merge_kernel,
        flops=20 * parts[0].size * len(parts),
        vmem_mb=8,
        in_specs=[SMEM] + [VMEM] * len(parts),
        out_specs=VMEM,
        out_shape=SDS(parts[0].shape, jnp.float32),
        scratch_shapes=[pltpu.VMEM((len(parts),) + parts[0].shape, jnp.float32)],
        name="merge",
    )(mine[None], *parts)


def groups(dom_count, row_count):
    flips = [(0, 1 << i) for i in range(row_count.bit_length() - 1)]
    flips += [(1 << i, 0) for i in range(dom_count.bit_length() - 1)]
    return [flips[:1]] + [flips[i : i + 2] for i in range(1, len(flips), 2)]


def exchange(value, group):
    parts = [value]
    for i in range(1, 1 << len(group)):
        picked = [flip for j, flip in enumerate(group) if i >> j & 1]
        parts.append(swap(value, sum(f[0] for f in picked), sum(f[1] for f in picked)))
    return parts


def exchange_stats(stats, dom_at, row_at, dom_count, row_count):
    rounds = groups(dom_count, row_count)
    for n, group in enumerate(rounds):
        mine = jnp.int32(0)
        for i, (d, r) in enumerate(group):
            bit = (row_at & r) != 0 if r else (dom_at & d) != 0
            mine = mine + (bit.astype(jnp.int32) << i)
        parts = exchange(stats, group)
        if n < len(rounds) - 1:
            stats = merge(mine, parts)
    return mine, parts


def pair_sum(value, group, *others):
    parts = exchange(hold(value, *others) if others else value, group)
    while len(parts) > 1:
        parts = [a + b for a, b in zip(parts[::2], parts[1::2])]
    return parts[0]


def backward_kernel(mine, params, mask_ref, cot_in, pre_in, *refs, first, part_count):
    parts = refs[:part_count]
    grad_pre, sums, output, ordered, cot_ref, pre_ref, out_ref, sems, out_sems = refs[-9:]
    rows, span = grad_pre.shape
    step = rows // 4
    there = pl.ds(first, span)
    copies, sent = [], []
    for n in range(4):
        here = pl.ds(n * step, step)
        copies += [
            pltpu.make_async_copy(pre_in.at[here, :], pre_ref.at[here, :], sems.at[0, n]),
            pltpu.make_async_copy(cot_in.at[here, there], cot_ref.at[here, :], sems.at[1, n]),
        ]
    for copy in copies:
        copy.start()
    mean, spread, shift_grad, scale_sum, count = merged(mine[0], parts, ordered)
    inverse = lax.rsqrt(spread / count + NORM_EPS)
    scale_grad = scale_sum * inverse
    scale, shift = params[1:2, :], params[2:3, :]
    gain = scale * inverse
    shift_mean, scale_mean = shift_grad / count, scale_grad / count
    for i, row in enumerate((scale_grad, shift_grad)):
        sums[i + 1 : i + 2, :] = row[:, first : first + span]
    sums[3:8, :] = jnp.zeros((5, span), jnp.float32)
    for n in range(4):
        for copy in copies[2 * n : 2 * n + 2]:
            copy.wait()
        at = slice(n * step, (n + 1) * step)
        mask = mask_ref[at, :]
        for part in range(span // LANES):
            here = slice(part * LANES, (part + 1) * LANES)
            of = slice(first + part * LANES, first + (part + 1) * LANES)
            v = pre_ref[at, here]
            bend = gelu_parts(v)
            act = 0.5 * v * (1.0 + bend)
            normed = (act - mean[:, of]) * inverse[:, of]
            out_ref[at, here] = (mask * (scale[:, of] * normed + shift[:, of])).astype(jnp.bfloat16)
            grad_out = mask * cot_ref[at, here].astype(jnp.float32)
            grad_act = (
                mask * gain[:, of] * (grad_out - shift_mean[:, of] - normed * scale_mean[:, of])
            )
            slope = 0.5 * (1.0 + bend) + 0.5 * v * (1.0 - bend * bend) * (
                GELU_ROOT * (1.0 + 3.0 * GELU_CUBE * (v * v))
            )
            low = (grad_act * slope).astype(jnp.bfloat16)
            grad_pre[at, here] = low
            total = jnp.sum(low.astype(jnp.float32), axis=0, keepdims=True)
            sums[0:1, here] = total if n == 0 else sums[0:1, here] + total
        here = pl.ds(n * step, step)
        sent.append(
            pltpu.make_async_copy(out_ref.at[here, :], output.at[here, there], out_sems.at[n])
        )
        sent[-1].start()
    for copy in sent:
        copy.wait()


def backward(mine, params, mask, cotangent, preact, parts, part, output):
    rows, span = preact.shape
    width = cotangent.shape[1]
    before = [] if output is None else [output]

    def kernel(*refs):
        backward_kernel(*refs, first=part * span, part_count=len(parts))

    return call(
        kernel,
        flops=50 * rows * span,
        vmem_mb=56,
        in_specs=[SMEM, VMEM, VMEM, ANY, ANY] + [VMEM] * len(parts) + [ANY] * len(before),
        out_specs=[VMEM, VMEM, ANY],
        out_shape=[
            SDS((rows, span), jnp.bfloat16),
            SDS((STAT_ROWS, span), jnp.float32),
            SDS((rows, width), jnp.bfloat16),
        ],
        scratch_shapes=[
            pltpu.VMEM((len(parts), STAT_ROWS, width), jnp.float32),
            pltpu.VMEM((rows, span), jnp.bfloat16),
            pltpu.VMEM((rows, span), jnp.float32),
            pltpu.VMEM((rows, span), jnp.bfloat16),
            pltpu.SemaphoreType.DMA((2, 4)),
            pltpu.SemaphoreType.DMA((4,)),
        ],
        input_output_aliases={5 + len(parts): 2} if before else {},
        name="backward",
    )(mine[None], params, mask, cotangent, preact, *parts, *before)


def outers_kernel(me, *refs):
    inputs, outputs, buffers = list(refs[:6]), refs[6:10], refs[10:16]
    low_ref, sems, out_sems = refs[16:]
    inputs[0] = inputs[0].at[0]
    copies = [
        pltpu.make_async_copy(source, buffer, sems.at[n])
        for n, (source, buffer) in enumerate(zip(inputs, buffers))
    ]
    for copy in copies:
        copy.start()
    own_flip, near_flip = buffers[:2]
    rows, span = buffers[2].shape
    half = rows // 2
    sent = []
    for part in range(2):
        for n in ((0, 1, 2, 3), (4, 5))[part]:
            copies[n].wait()
        grad, near_grad = buffers[2 + 2 * part : 4 + 2 * part]
        for c in range(span // COLS):
            cs = slice(c * COLS, (c + 1) * COLS)
            total = dot(own_flip[...], grad[:, cs]) + dot(near_flip[...], near_grad[:, cs])
            low_ref[part, :, cs] = total.astype(jnp.bfloat16)
        for n in range(2):
            here = pl.ds(n * half, half)
            if part:
                kept, given = (
                    pl.multiple_of(n * rows + flag * half, half) for flag in (me[2], 1 - me[2])
                )
            else:
                kept, given = n * half, rows + n * half
            for m, start in enumerate((kept, given)):
                sent.append(
                    pltpu.make_async_copy(
                        low_ref.at[part, pl.ds(start, half), :],
                        outputs[2 * part + m].at[here, :],
                        out_sems.at[part, m, n],
                    )
                )
                sent[-1].start()
    for copy in sent:
        copy.wait()


def outers(me, hidden_flip, near_flip, grads, near_grads):
    rows, span = grads[0].shape
    low = jnp.bfloat16
    inputs = [hidden_flip, near_flip, grads[0], near_grads[0], grads[1], near_grads[1]]
    return call(
        outers_kernel,
        flops=0,
        vmem_mb=56,
        in_specs=[SMEM] + [ANY] * 6,
        out_specs=[ANY] * 4,
        out_shape=[SDS((rows, span), low)] * 4,
        scratch_shapes=[pltpu.VMEM(v.shape[-2:], low) for v in inputs]
        + [
            pltpu.VMEM((2, 2 * rows, span), low),
            pltpu.SemaphoreType.DMA((6,)),
            pltpu.SemaphoreType.DMA((2, 2, 2)),
        ],
        name="outers",
    )(me, *inputs)


def hidden_kernel(me, *refs, piece_total, slot_total, halved):
    inputs, refs = refs[: 3 + piece_total], refs[3 + piece_total :]
    outputs, refs = refs[: 1 + slot_total], refs[1 + slot_total :]
    buffers, refs = refs[: 3 + piece_total], refs[3 + piece_total :]
    grad_hidden, slots, sems, out_sem, slot_sems = refs
    grads, weights, halo_flip = buffers[:2], buffers[2:-1], buffers[-1]
    copies = [
        pltpu.make_async_copy(source, buffer, sems.at[n])
        for n, (source, buffer) in enumerate(zip(inputs, buffers))
    ]
    for copy in copies:
        copy.start()
    rows, width = grad_hidden.shape
    span = grads[0].shape[1]
    for copy in copies[:2]:
        copy.wait()
    for start, ref, copy in zip(weight_starts(me, rows), weights, copies[2:]):
        copy.wait()
        for c in range(ref.shape[0] // COLS):
            total = sum(
                dot(
                    grad[...],
                    ref[c * COLS : (c + 1) * COLS, p * span : (p + 1) * span],
                    BOTH_LAST,
                )
                for p, grad in enumerate(grads)
            )
            at = pl.multiple_of(start + c * COLS, COLS)
            grad_hidden[:, pl.ds(at, COLS)] = total.astype(jnp.bfloat16)
    out_copy = pltpu.make_async_copy(grad_hidden, outputs[0], out_sem)
    out_copy.start()
    copies[-1].wait()
    side = slots.shape[1] // SLOT_GROUP
    count = halo_flip.shape[0] // side - 1
    targets = list(outputs[1:])
    pending = {}
    for first in range(0, count, SLOT_GROUP):
        taken = min(SLOT_GROUP, count - first)
        buffer = first // SLOT_GROUP % 2
        for copy in pending.pop(buffer, ()):
            copy.wait()
        for c in range(width // COLS):
            cs = slice(c * COLS, (c + 1) * COLS)
            picked = halo_flip[(first + 1) * side : (first + 1 + taken) * side, :]
            slots[buffer, : taken * side, cs] = dot(picked, grad_hidden[:, cs]).astype(jnp.bfloat16)
        pending[buffer] = []
        for n in range(taken):
            for part in range(2 if first + n + 1 in halved else 1):
                target = targets.pop(0)
                height = target.shape[0]
                pending[buffer].append(
                    pltpu.make_async_copy(
                        slots.at[buffer, pl.ds(n * side + part * height, height), :],
                        target,
                        slot_sems.at[buffer, n, part],
                    )
                )
                pending[buffer][-1].start()
    for copy in sum(pending.values(), [out_copy]):
        copy.wait()


def hidden_grads(me, grads, weights, halo_flip, side, halved):
    rows, span = grads[0].shape
    width = 2 * span
    count = halo_flip.shape[0] // side - 1
    low = jnp.bfloat16
    shapes = []
    for k in range(1, count + 1):
        shapes += [SDS((side // 2, width), low)] * 2 if k in halved else [SDS((side, width), low)]
    inputs = [*grads, *weights, halo_flip]

    def kernel(*refs):
        hidden_kernel(*refs, piece_total=len(weights), slot_total=len(shapes), halved=halved)

    grad_hidden, *outs = call(
        kernel,
        flops=0,
        vmem_mb=56,
        in_specs=[SMEM] + [ANY] * len(inputs),
        out_specs=[ANY] * (1 + len(shapes)),
        out_shape=[SDS((rows, width), low)] + shapes,
        scratch_shapes=[pltpu.VMEM(v.shape, low) for v in inputs]
        + [
            pltpu.VMEM((rows, width), low),
            pltpu.VMEM((2 if count > SLOT_GROUP else 1, SLOT_GROUP * side, width), low),
            pltpu.SemaphoreType.DMA((len(inputs),)),
            pltpu.SemaphoreType.DMA,
            pltpu.SemaphoreType.DMA((2, SLOT_GROUP, 2)),
        ],
        name="hidden_grads",
    )(me, *inputs)
    slots = {}
    for k in range(1, count + 1):
        for part in range(2 if k in halved else 1):
            slots[k, part] = outs.pop(0)
    return grad_hidden, slots


def pieces_of(chooser, numbers, side):
    return [chooser[:, (k - 1) * side : k * side] for k in numbers]


def near_back(flips, grads, chooser, returned):
    rows, width = grads[0].shape
    numbers, blocks = sorted(returned), [returned[k] for k in sorted(returned)]
    side = blocks[0].shape[0]

    def kernel(*refs):
        flips_in, refs = refs[: len(flips)], refs[len(flips) :]
        grads_in, refs = refs[: len(grads)], refs[len(grads) :]
        chooser_ref, blocks_in, out = refs[0], refs[1:-1], refs[-1]
        picked = jnp.concatenate(pieces_of(chooser_ref, numbers, side), axis=1)
        for c in range(width // COLS):
            cs = slice(c * COLS, (c + 1) * COLS)
            total = dot(picked, jnp.concatenate([block[:, cs] for block in blocks_in], axis=0))
            done = 0
            for grad in grads_in:
                depth = grad.shape[0]
                flip = flips_in[done // rows]
                total += dot(flip[:, done % rows : done % rows + depth], grad[:, cs])
                done += depth
            out[:, cs] = total

    blocked = chooser.shape[1] > WHOLE_HALO
    if blocked:
        grid, block, whole = columns(width, True)
        specs = [whole((rows, rows))] * len(flips) + [block(g.shape[0]) for g in grads]
        specs += [whole(chooser.shape)] + [block(side)] * len(blocks)
        width = COLS
    else:
        grid, specs = {}, [VMEM] * (len(flips) + len(grads) + 1 + len(blocks))
    return call(
        kernel,
        flops=0,
        vmem_mb=56,
        in_specs=specs,
        out_specs=block(rows) if blocked else VMEM,
        out_shape=SDS((rows, grads[0].shape[1]), jnp.float32),
        name="near_back",
        **grid,
    )(*flips, *grads, chooser, *blocks)


def give_back(chooser, base, returned):
    rows, width = base.shape
    numbers, blocks = sorted(returned), [returned[k] for k in sorted(returned)]
    side = blocks[0].shape[0]
    blocked = chooser.shape[1] > WHOLE_HALO
    grid, block, whole = columns(width, blocked)

    def kernel(chooser_ref, base_ref, *refs):
        blocks_in, out = refs[:-1], refs[-1]
        picked = jnp.concatenate(pieces_of(chooser_ref, numbers, side), axis=1)
        for c in range(out.shape[1] // COLS):
            cs = slice(c * COLS, (c + 1) * COLS)
            pieces = jnp.concatenate([block[:, cs] for block in blocks_in], axis=0)
            out[:, cs] = (base_ref[:, cs] + dot(picked, pieces)).astype(jnp.bfloat16)

    return call(
        kernel,
        flops=0,
        vmem_mb=56,
        in_specs=[whole(chooser.shape), block(rows)] + [block(side)] * len(blocks),
        out_specs=block(rows),
        out_shape=SDS((rows, width), jnp.bfloat16),
        name="give_back",
        **grid,
    )(chooser, base, *blocks)


def lamb_step(value, grad, first, second, decay):
    first_new = DECAY_FIRST * first + (1.0 - DECAY_FIRST) * grad
    second_new = DECAY_SECOND * second + (1.0 - DECAY_SECOND) * grad * grad
    update = (
        first_new
        / (1.0 - DECAY_FIRST**STEP)
        / (jnp.sqrt(second_new / (1.0 - DECAY_SECOND**STEP)) + ADAM_EPS)
        + decay * value
    )
    return (first_new, second_new, update)


def term_sum(terms):
    return sum(term[...].astype(jnp.float32) for term in terms)


def first_sends(side_bit, keep_a, came_a, keep_b, came_b):
    rows, span = keep_a.shape
    half = rows // 2
    block = lambda place: pl.BlockSpec((half, span), place)
    other, second = block(lambda i, bit: (1 - bit[0], 0)), block(lambda i, bit: (1, 0))

    def kernel(bit, *refs):
        for n, out in enumerate(refs[4:]):
            out[...] = term_sum(refs[2 * n : 2 * n + 2]).astype(out.dtype)

    return call(
        kernel,
        flops=0,
        vmem_mb=56,
        grid_spec=pltpu.PrefetchScalarGridSpec(
            num_scalar_prefetch=1,
            grid=(1,),
            in_specs=[other] * 2 + [second] * 2,
            out_specs=[block(lambda i, bit: (0, 0))] * 2,
        ),
        out_shape=[SDS((half, span), jnp.bfloat16)] * 2,
        name="first_sends",
    )(side_bit[None], keep_a, came_a, keep_b, came_b)


def rows_sum(start, rows, terms_a, terms_b, terms, extra=()):
    span = terms_a[0][0].shape[1]
    narrow = [*terms_a, *terms_b]
    places = jnp.stack([(start - offset) // rows for _, offset in [*narrow, *terms]]).astype(jnp.int32)
    at = lambda n, cols: pl.BlockSpec((rows, cols), lambda i, places: (places[n], 0))
    specs = [at(n, span) for n in range(len(narrow))]
    specs += [at(len(narrow) + n, 2 * span) for n in range(len(terms))]
    return places, specs, [term for term, _ in [*narrow, *terms]], len(terms_a), len(narrow)


def send_rows(start, rows, terms_a, terms_b, terms):
    places, specs, arrays, cut, narrow = rows_sum(start, rows, terms_a, terms_b, terms)
    span = arrays[0].shape[1]

    def kernel(places, *refs):
        out = refs[-1]
        wide = term_sum(refs[narrow:-1])
        for n, part in enumerate((refs[:cut], refs[cut:narrow])):
            cs = slice(n * span, (n + 1) * span)
            more = wide if isinstance(wide, int) else wide[:, cs]
            out[:, cs] = (term_sum(part) + more).astype(out.dtype)

    return call(
        kernel,
        flops=0,
        vmem_mb=56,
        grid_spec=pltpu.PrefetchScalarGridSpec(
            num_scalar_prefetch=1,
            grid=(1,),
            in_specs=specs,
            out_specs=pl.BlockSpec((rows, 2 * span), lambda i, places: (0, 0)),
        ),
        out_shape=SDS((rows, 2 * span), jnp.bfloat16),
        name="send_rows",
    )(places, *arrays)


def piece_totals(start, rows, terms_a, terms_b, terms, sums, weight, first, second):
    places, specs, arrays, cut, narrow = rows_sum(start, rows, terms_a, terms_b, terms)
    span = arrays[0].shape[1]
    own = pl.BlockSpec((rows, 2 * span), lambda i, places: (places[0], 0))
    whole = lambda height: pl.BlockSpec((height, 2 * span), lambda i, places: (0, 0))

    def kernel(places, *refs):
        sums, value, first, second, piece, totals = refs[-6:]
        wide = term_sum(refs[narrow:-6])
        totals[0:1, :] = sums[0:1, :]
        totals[3:8, :] = jnp.zeros((5, 2 * span), jnp.float32)
        for n, part in enumerate((refs[:cut], refs[cut:narrow])):
            cs = slice(n * span, (n + 1) * span)
            low = (term_sum(part) + wide[:, cs]).astype(jnp.bfloat16)
            piece[:, cs] = low
            update = lamb_step(
                value[:, cs], low.astype(jnp.float32), first[:, cs], second[:, cs], WEIGHT_DECAY
            )[2]
            totals[1:2, cs] = jnp.sum(value[:, cs] * value[:, cs], axis=0, keepdims=True)
            totals[2:3, cs] = jnp.sum(update * update, axis=0, keepdims=True)

    return call(
        kernel,
        flops=0,
        vmem_mb=56,
        grid_spec=pltpu.PrefetchScalarGridSpec(
            num_scalar_prefetch=1,
            grid=(1,),
            in_specs=specs + [whole(STAT_ROWS)] + [own] * 3,
            out_specs=[whole(rows), whole(STAT_ROWS)],
        ),
        out_shape=[SDS((rows, 2 * span), jnp.bfloat16), SDS((STAT_ROWS, 2 * span), jnp.float32)],
        name="piece_totals",
    )(places, *arrays, sums, weight, first, second)


def by_bit(flag, own, came):
    rows, width = own.shape
    mine = (jnp.arange(2, dtype=jnp.int32) == flag)[:, None, None]
    return jnp.where(mine, own[None], came[None]).reshape(2 * rows, width)


def on_device(
    features,
    adjacency,
    tile_values,
    tile_block,
    tile_slot,
    tile_count,
    send_block,
    node_mask,
    weight,
    params,
    weight_first,
    weight_second,
    params_first,
    params_second,
    cotangent,
):
    dom_count, row_count = lax.axis_size("dom"), lax.axis_size("row")
    dom_at, row_at = lax.axis_index("dom"), lax.axis_index("row")
    rows, width = features.shape
    side = tile_values.shape[1]
    side_bit = dom_at % 2
    me = jnp.stack([dom_at, row_at, side_bit]).astype(jnp.int32)
    sends = send_block[0]
    mask = jnp.broadcast_to(node_mask.astype(jnp.float32)[:, None], (rows, LANES))

    half = rows // 2
    low_weight = weight.astype(jnp.bfloat16)
    first_half, second_half, blocks = outgoing(me, sends, features, side)
    wide, flip, halo, halo_flip, chooser = prepare(
        me, sends, tile_block, tile_slot, tile_count, adjacency, tile_values, dom_count
    )

    far, light = turns(dom_count)
    arrived = {}
    whole = lambda order: [(k, 0) for k in order]
    out = lambda key: blocks[key[0] - 1]
    far_first = swap(first_half, 0, 2)
    near_features = swap(features, 0, 1)
    turn = [
        far_first,
        near_features,
        send_in_turn(out, whole(far[0]), arrived),
        send_in_turn(out, whole(light[0]), arrived),
    ]
    far_second = swap(hold(second_half, *turn), 0, 2)
    cross = [swap(hold(far_first, *turn), 0, 1)]
    turn = [
        far_second,
        cross[0],
        send_in_turn(out, whole(far[1]), arrived, *turn),
        send_in_turn(out, whole(light[1]), arrived, *turn),
    ]
    over_y = swap(hold(low_weight[:half], *turn), 0, 2)
    cross.append(swap(hold(far_second, *turn), 0, 1))
    near_weight = swap(hold(low_weight, *turn), 0, 1)
    turn = [
        over_y,
        cross[1],
        near_weight,
        send_in_turn(out, whole(far[2]), arrived, *turn),
        send_in_turn(out, whole(light[2]), arrived, *turn),
    ]
    over_y_too = swap(hold(low_weight[half:], *turn), 0, 2)
    send_in_turn(out, whole(far[3]), arrived, *turn)
    base = near(wide, [features, near_features, far_first, far_second] + cross)
    weights = [
        low_weight,
        near_weight,
        over_y,
        over_y_too,
        swap(hold(over_y, base), 0, 1),
        swap(over_y_too, 0, 1),
    ]
    arrived = [arrived[k, 0] for k in range(1, dom_count)]
    hidden, hidden_flip = add_halo(me, base, halo, arrived, row_count)
    pre_first, pre_second, stats = linear(me, hidden, params, mask, cotangent, weights)
    mine, parts = exchange_stats(stats, dom_at, row_at, dom_count, row_count)
    near_flip = swap(hidden_flip[1], 0, 1)

    mine = hold(mine, near_flip)
    output, grads, near_pre, sums = None, [], [], []
    for part, preact in enumerate((pre_first, pre_second)):
        grad_pre, sum_part, output = backward(
            mine, params, mask, cotangent, preact, parts, part, output
        )
        grads.append(grad_pre)
        near_pre.append(swap(grad_pre, 0, 1))
        sums.append(sum_part)
    sums = jnp.concatenate(sums, axis=1)
    halved = []
    keep_a, send_a, keep_b, send_b = outers(me, hidden_flip, near_flip, grads, near_pre)
    grad_hidden, slots = hidden_grads(me, grads, weights, halo_flip, side, halved)

    returned = {}
    part_of = lambda order, n: [(k, n) for k in order]
    bit = lambda step: (dom_at // step) % 2
    blocks_back = lambda order, *turn: send_in_turn(lambda k: slots[k], order, returned, *turn)

    turn_flip = lambda j, *turn: swap(hold(flip[j * rows : (j + 1) * rows], *turn), 0, j)
    rounds = groups(dom_count, row_count)

    small_steps = sum(rounds, [])

    flips = [flip[:rows], turn_flip(1, send_a), None, None]
    turn = [swap(send_a, 0, 2), swap(send_b, 1, 0), flips[1], grad_hidden]
    sent_a, sent_b = first_sends(side_bit, keep_a, turn[0], keep_b, turn[1])
    terms_a, terms_b, terms = [(keep_a, 0), (turn[0], 0)], [(keep_b, side_bit * half), (turn[1], side_bit * half)], []
    near_grad = swap(hold(grad_hidden, *turn), 0, 1)
    flips[2] = turn_flip(2, *turn)
    turn = [
        swap(hold(sent_a, *turn), 1, 0),
        swap(hold(sent_b, *turn), 0, 2),
        blocks_back(whole(far[0]), *turn),
        near_grad,
        flips[2],
    ]
    first, span = side_bit * half, half
    terms_a.append((turn[0], first))
    terms_b.append((turn[1], first))
    steps = [1 << n for n in range(1, dom_count.bit_length() - 1)]
    quarter = rows // 4
    grad_parts, cross = [], []

    def over_y_back(*turn):
        n = len(grad_parts)
        grad_parts.append(
            swap(hold(grad_hidden[n * quarter : (n + 1) * quarter], *turn), 0, 2)
        )
        more = [grad_parts[n]]
        if n > 1:
            cross.append(swap(hold(grad_parts[n - 2], *turn), 0, 1))
            more.append(cross[n - 2])
        if n == 1:
            flips[3] = turn_flip(3, *turn)
            more.append(flips[3])
        return more

    beside = [
        [whole(far[2]), whole(light[0])],
        [whole(light[1])],
        [],
        [whole(far[3])],
    ]
    for n, step in enumerate(steps):
        span //= 2
        sent = send_rows(first + (1 - bit(step)) * span, span, terms_a, terms_b, terms)
        first = first + bit(step) * span
        came = swap(hold(sent, *turn), step, 0)
        terms.append((came, first))
        more = []
        if n < 2:
            more = [blocks_back(order, *turn) for order in beside[n]] + over_y_back(*turn)
        turn = [came] + more
    weight_grad, totals = piece_totals(
        first, span, terms_a, terms_b, terms, sums, weight, weight_first, weight_second
    )
    for n, step in enumerate(reversed(steps)):
        came = swap(hold(weight_grad, *turn), step, 0)
        more = []
        if n < 2:
            more = [blocks_back(order, *turn) for order in beside[2 + n]] + over_y_back(*turn)
            for flip_bits in small_steps[:3] if n == 0 else small_steps[3:]:
                totals = pair_sum(totals, [flip_bits], *turn)
            more.append(totals)
        weight_grad = by_bit(bit(step), weight_grad, came)
        turn = [came] + more
    came = swap(hold(weight_grad, *turn), 1, 0)
    blocks_back(whole(far[1]), *turn)
    blocks_back(whole(light[2]), *turn)
    cross += [swap(hold(part, *turn), 0, 1) for part in grad_parts[-2:]]
    bias_grad = totals[0:1]
    weight_norms = jnp.sqrt(jnp.sum(totals[1:3], axis=1))
    late = far[1] + light[2]
    base = near_back(
        flips,
        [grad_hidden, near_grad] + grad_parts + cross,
        chooser,
        {key[0]: value for key, value in returned.items() if key[0] not in late},
    )
    weight_grad = by_bit(bit(1), weight_grad, hold(came, base)).astype(jnp.float32)
    returned = {key[0]: value for key, value in returned.items() if key[0] in late}
    weight_first_new, weight_second_new, weight_update = lamb_step(
        weight, weight_grad, weight_first, weight_second, WEIGHT_DECAY
    )
    weight_new = (
        weight - LEARN_RATE * (weight_norms[0] / (weight_norms[1] + TRUST_EPS)) * weight_update
    )

    grad_features = give_back(chooser, hold(base, weight_new), returned)
    param_grads = jnp.concatenate([bias_grad, sums[1:3]], axis=0)
    params_first_new, params_second_new, param_update = lamb_step(
        params, param_grads, params_first, params_second, 0.0
    )
    param_norms = jnp.sqrt(jnp.sum(params * params, axis=1, keepdims=True))
    update_norms = jnp.sqrt(jnp.sum(param_update * param_update, axis=1, keepdims=True))
    params_new = params - LEARN_RATE * (param_norms / (update_norms + TRUST_EPS)) * param_update
    norms = jnp.concatenate(
        [weight_norms[None, :], jnp.concatenate([param_norms, update_norms], axis=1)], axis=0
    )
    return (
        output,
        grad_features,
        weight_new,
        weight_new.astype(jnp.bfloat16),
        weight_first_new,
        weight_second_new,
        params_new,
        params_first_new,
        params_second_new,
        norms,
    )


def solution(mesh):
    in_specs = (
        P(("dom", "row"), None),
        P(("dom", "row"), None),
        P(("dom", "row"), None, None),
        P(("dom", "row")),
        P(("dom", "row")),
        P(("dom", "row")),
        P(("dom", "row"), None),
        P(("dom", "row")),
        P("row", None),
        P(),
        P("row", None),
        P("row", None),
        P(),
        P(),
        P(("dom", "row"), None),
    )
    out_specs = (
        P(("dom", "row"), None),
        P(("dom", "row"), None),
        P("row", None),
        P("row", None),
        P("row", None),
        P("row", None),
        P(),
        P(),
        P(),
        P(),
    )
    return jax.shard_map(
        on_device, mesh=mesh, in_specs=in_specs, out_specs=out_specs, check_vma=False
    )
```

```python
import math

import jax
import jax.numpy as jnp
from jax import lax
from jax.experimental import pallas as pl
from jax.experimental.pallas import tpu as pltpu
from jax.sharding import PartitionSpec as P

STEP = 5


SELF_LOOP = 1.0
NORM_EPS = 1e-05
DECAY_FIRST = 0.5
DECAY_SECOND = 0.5
ADAM_EPS = 1e-06
WEIGHT_DECAY = 0.01
LEARN_RATE = 0.5
TRUST_EPS = 1e-06

AXES = ("dom", "row")
GELU_ROOT = math.sqrt(2.0 / math.pi)
GELU_CUBE = 0.044715
STAT_ROWS = 8
LANES = 128
COLS = 256
WHOLE_HALO = 2048
SLOT_GROUP = 7

ANY_ROWS = (((1,), (0,)), ((), ()))
BOTH_LAST = (((1,), (1,)), ((), ()))
SMEM = pl.BlockSpec(memory_space=pltpu.SMEM)
VMEM = pl.BlockSpec(memory_space=pltpu.VMEM)
ANY = pl.BlockSpec(memory_space=pl.ANY)
SDS = jax.ShapeDtypeStruct


def dot(left, right, dims=ANY_ROWS):
    return lax.dot_general(left, right, dims, preferred_element_type=jnp.float32)


def swap(value, dom_flip, row_flip):
    dom_count, row_count = lax.axis_size("dom"), lax.axis_size("row")
    pairs = [
        (d * row_count + r, (d ^ dom_flip) * row_count + (r ^ row_flip))
        for d in range(dom_count)
        for r in range(row_count)
    ]
    return lax.ppermute(value, AXES, pairs)


def hold(value, *others):
    return lax.optimization_barrier((value, *others))[0]


def call(kernel, *, flops, vmem_mb=56, **kw):
    return pl.pallas_call(
        kernel,
        cost_estimate=pl.CostEstimate(flops=int(flops), bytes_accessed=0, transcendentals=0),
        compiler_params=pltpu.CompilerParams(vmem_limit_bytes=vmem_mb << 20),
        **kw,
    )


def columns(width, blocked):
    if not blocked:
        return {}, lambda height: VMEM, lambda shape: VMEM
    grid = {"grid": (width // COLS,)}
    block = lambda height: pl.BlockSpec((height, COLS), lambda i: (0, i))
    whole = lambda shape: pl.BlockSpec(shape, lambda i: (0,) * len(shape))
    return grid, block, whole


def turns(dom_count):
    half = dom_count // 2
    far = sorted(range(half, dom_count), key=lambda k: (k % 2, k if k % 2 else -k))
    near = sorted(range(1, half), key=lambda k: (k % 2 == 0, k))
    cut = lambda order, n, of: order[n * len(order) // of : (n + 1) * len(order) // of]
    return [cut(far, n, 4) for n in range(4)], [cut(near, n, 3) for n in range(3)]


def send_in_turn(piece, order, arrived, *first):
    for key in order:
        value = hold(piece(key), *first) if first else piece(key)
        arrived[key] = swap(value, key[0], 0)
        first = (arrived[key],)
    return first[0]


def prepare_kernel(
    me, sends, block_ref, slot_ref, count_ref, adj_ref, tile_ref, *refs
):
    wide, flip, halo, halo_flip, chooser, total = refs
    rows = adj_ref.shape[0]
    row_count = adj_ref.shape[1] // rows
    blocks, peers, side = total.shape[0], total.shape[1], total.shape[2]
    for j in range(row_count):
        start = pl.multiple_of((me[1] ^ j) * rows, rows)
        piece = adj_ref[:, pl.ds(start, rows)]
        if j == 0:
            at_row = lax.broadcasted_iota(jnp.int32, (rows, rows), 0)
            at_col = lax.broadcasted_iota(jnp.int32, (rows, rows), 1)
            wide_piece = piece.astype(jnp.float32)
            piece = jnp.where(at_row == at_col, (1.0 + SELF_LOOP) * wide_piece, wide_piece).astype(
                jnp.bfloat16
            )
        wide[:, j * rows : (j + 1) * rows] = piece
        flip[j * rows : (j + 1) * rows, :] = piece.T
    total[...] = jnp.zeros(total.shape, total.dtype)

    def add(t, carry):
        b = block_ref[t]
        k = slot_ref[t] ^ me[0]
        total[b, k] = total[b, k] + tile_ref[t].astype(jnp.float32)
        return carry

    lax.fori_loop(0, count_ref[0], add, 0)
    for b in range(blocks):
        for k in range(peers):
            piece = total[b, k].astype(jnp.bfloat16)
            halo[b * side : (b + 1) * side, k * side : (k + 1) * side] = piece
            halo_flip[k * side : (k + 1) * side, b * side : (b + 1) * side] = piece.T
    same = lax.broadcasted_iota(jnp.int32, (side, side), 0) == lax.broadcasted_iota(
        jnp.int32, (side, side), 1
    )
    for k in range(peers - 1):
        for b in range(blocks):
            chooser[b * side : (b + 1) * side, k * side : (k + 1) * side] = jnp.where(
                jnp.logical_and(same, sends[me[0] ^ (k + 1)] == b), 1.0, 0.0
            ).astype(jnp.bfloat16)


def prepare(me, sends, tile_block, tile_slot, tile_count, adjacency, tiles, peers):
    rows, part = adjacency.shape
    side = tiles.shape[1]
    bf = jnp.bfloat16
    return call(
        prepare_kernel,
        flops=tiles.size,
        vmem_mb=20 + (10 * rows * peers * side >> 20),
        in_specs=[SMEM] * 5 + [VMEM] * 2,
        out_specs=[VMEM] * 5,
        out_shape=[
            SDS((rows, part), bf),
            SDS((part, rows), bf),
            SDS((rows, peers * side), bf),
            SDS((peers * side, rows), bf),
            SDS((rows, (peers - 1) * side), bf),
        ],
        scratch_shapes=[pltpu.VMEM((rows // side, peers, side, side), jnp.float32)],
        name="prepare",
    )(me, sends, tile_block, tile_slot, tile_count, adjacency, tiles)


def outgoing_kernel(me, sends, source, *targets):
    halves, blocks = targets[:2], targets[2:]
    rows, side = halves[0].shape[0], blocks[0].shape[0]
    for n, target in enumerate(halves):
        target[...] = source[n * rows : (n + 1) * rows, :]
    for k, target in enumerate(blocks):
        block = jnp.maximum(sends[me[0] ^ (k + 1)], 0)
        target[...] = source[pl.ds(pl.multiple_of(block * side, side), side), :]


def outgoing(me, sends, features, side):
    rows, width = features.shape
    count = sends.shape[0] - 1
    low = features.dtype
    first, second, *blocks = call(
        outgoing_kernel,
        flops=0,
        vmem_mb=12 + (count * side * width >> 19),
        in_specs=[SMEM, SMEM, VMEM],
        out_specs=[VMEM] * (2 + count),
        out_shape=[SDS((rows // 2, width), low)] * 2 + [SDS((side, width), low)] * count,
        name="outgoing",
    )(me, sends, features)
    return first, second, blocks


def near_kernel(wide, *refs):
    sources, out = refs[:-1], refs[-1]
    for c in range(out.shape[1] // COLS):
        cs = slice(c * COLS, (c + 1) * COLS)
        total, done = 0.0, 0
        for ref in sources:
            total += dot(wide[:, done : done + ref.shape[0]], ref[:, cs])
            done += ref.shape[0]
        out[:, cs] = total


def near(wide, sources):
    rows, width = sources[0].shape
    return call(
        near_kernel,
        flops=2 * wide.size * width,
        vmem_mb=16,
        in_specs=[VMEM] * (1 + len(sources)),
        out_specs=VMEM,
        out_shape=SDS((rows, width), jnp.float32),
        name="near",
    )(wide, *sources)


def halo_kernel(me, base, halo, *refs, row_count, blocked):
    arrived, (hidden, hidden_flip) = refs[:-2], refs[-2:]
    rows, side = hidden.shape[0], arrived[0].shape[0]
    per = rows // COLS
    count = base.shape[1] // COLS
    for c in range(count):
        cs = slice(c * COLS, (c + 1) * COLS)
        at = c + (pl.program_id(0) * count if blocked else 0)
        pieces = jnp.concatenate([ref[:, cs] for ref in arrived], axis=0)
        low = (base[:, cs] + dot(halo[:, side:], pieces)).astype(jnp.bfloat16)
        hidden[:, pl.ds(pl.multiple_of(at * COLS, COLS), COLS)] = low
        j = (at // per) ^ me[1]
        start = pl.multiple_of(j // 2 * rows + at % per * COLS, COLS)
        hidden_flip[j % 2, pl.ds(start, COLS), :] = low.T


def add_halo(me, base, halo, arrived, row_count):
    rows, width = base.shape
    blocked = halo.shape[1] > WHOLE_HALO
    grid, block, whole = columns(width, blocked)

    def kernel(*refs):
        halo_kernel(*refs, row_count=row_count, blocked=blocked)

    return call(
        kernel,
        flops=2 * halo.size * width,
        vmem_mb=56 if blocked else 16,
        in_specs=[SMEM, block(rows), whole(halo.shape)]
        + [block(a.shape[0]) for a in arrived],
        out_specs=[whole((rows, width)), whole((2, width // 2, rows))],
        out_shape=[SDS((rows, width), jnp.bfloat16), SDS((2, width // 2, rows), jnp.bfloat16)],
        name="add_halo",
        **grid,
    )(me, base, halo, *arrived)


def gelu_parts(v):
    inner = GELU_ROOT * (v + GELU_CUBE * (v * v * v))
    return jnp.tanh(inner)


def weight_starts(me, rows):
    half = rows // 2
    starts = [me[1] * rows, (me[1] ^ 1) * rows]
    for j in (2, 3):
        starts += [(me[1] ^ j) * rows, (me[1] ^ j) * rows + half]
    return [pl.multiple_of(start, half) for start in starts]


def linear_kernel(me, hidden, params, mask_ref, cot_ref, *refs):
    weights, (pre_first, pre_second, stats, act_ref) = refs[:-4], refs[-4:]
    rows, width = hidden.shape
    starts = weight_starts(me, rows)
    mask = mask_ref[...]
    count = jnp.sum(mask[:, 0:1])
    stats[4:8, :] = jnp.full((4, width), count, jnp.float32)
    for c in range(width // COLS):
        cs = slice(c * COLS, (c + 1) * COLS)
        v = params[0:1, cs] + sum(
            dot(hidden[:, pl.ds(start, ref.shape[0])], ref[:, cs])
            for start, ref in zip(starts, weights)
        )
        span = width // 2
        preact = pre_second if c * COLS >= span else pre_first
        preact[:, c * COLS % span : c * COLS % span + COLS] = v
        act_ref[...] = 0.5 * v * (1.0 + gelu_parts(v))
        for part in range(COLS // LANES):
            here = slice(part * LANES, (part + 1) * LANES)
            there = slice(c * COLS + part * LANES, c * COLS + (part + 1) * LANES)
            act = act_ref[:, here]
            mean = jnp.sum(mask * act, axis=0, keepdims=True) / count
            centred = act - mean
            grad = mask * cot_ref[:, there].astype(jnp.float32)
            stats[0:1, there] = mean
            stats[1:2, there] = jnp.sum(mask * centred * centred, axis=0, keepdims=True)
            stats[2:3, there] = jnp.sum(grad, axis=0, keepdims=True)
            stats[3:4, there] = jnp.sum(grad * centred, axis=0, keepdims=True)


def linear(me, hidden, params, mask, cotangent, weights):
    rows, width = hidden.shape
    return call(
        linear_kernel,
        flops=2 * rows * width * width,
        vmem_mb=16,
        in_specs=[SMEM] + [VMEM] * (4 + len(weights)),
        out_specs=[VMEM] * 3,
        out_shape=[SDS((rows, width // 2), jnp.float32)] * 2
        + [SDS((STAT_ROWS, width), jnp.float32)],
        scratch_shapes=[pltpu.VMEM((rows, COLS), jnp.float32)],
        name="linear",
    )(me, hidden, params, mask, cotangent, *weights)


def merged(mine, refs, ordered):
    for i, ref in enumerate(refs):
        ordered[mine ^ i] = ref[...]
    parts = [ordered[i] for i in range(len(refs))]
    count = sum(p[4:5] for p in parts)
    mean = sum(p[4:5] * p[0:1] for p in parts) / count
    spread = sum(p[1:2] + p[4:5] * (p[0:1] - mean) * (p[0:1] - mean) for p in parts)
    shift = sum(p[2:3] for p in parts)
    scale = sum(p[3:4] + (p[0:1] - mean) * p[2:3] for p in parts)
    return mean, spread, shift, scale, count


def merge_kernel(mine, *refs):
    out, ordered = refs[-2:]
    for i, row in enumerate(merged(mine[0], refs[:-2], ordered)):
        out[i : i + 1, :] = row
    out[5:8, :] = jnp.zeros((3, out.shape[1]), jnp.float32)


def merge(mine, parts):
    return call(
        merge_kernel,
        flops=20 * parts[0].size * len(parts),
        vmem_mb=8,
        in_specs=[SMEM] + [VMEM] * len(parts),
        out_specs=VMEM,
        out_shape=SDS(parts[0].shape, jnp.float32),
        scratch_shapes=[pltpu.VMEM((len(parts),) + parts[0].shape, jnp.float32)],
        name="merge",
    )(mine[None], *parts)


def groups(dom_count, row_count):
    flips = [(0, 1 << i) for i in range(row_count.bit_length() - 1)]
    flips += [(1 << i, 0) for i in range(dom_count.bit_length() - 1)]
    return [flips[:1]] + [flips[i : i + 2] for i in range(1, len(flips), 2)]


def exchange(value, group):
    parts = [value]
    for i in range(1, 1 << len(group)):
        picked = [flip for j, flip in enumerate(group) if i >> j & 1]
        parts.append(swap(value, sum(f[0] for f in picked), sum(f[1] for f in picked)))
    return parts


def exchange_stats(stats, dom_at, row_at, dom_count, row_count):
    rounds = groups(dom_count, row_count)
    for n, group in enumerate(rounds):
        mine = jnp.int32(0)
        for i, (d, r) in enumerate(group):
            bit = (row_at & r) != 0 if r else (dom_at & d) != 0
            mine = mine + (bit.astype(jnp.int32) << i)
        parts = exchange(stats, group)
        if n < len(rounds) - 1:
            stats = merge(mine, parts)
    return mine, parts


def pair_sum(value, group, *others):
    parts = exchange(hold(value, *others) if others else value, group)
    while len(parts) > 1:
        parts = [a + b for a, b in zip(parts[::2], parts[1::2])]
    return parts[0]


def backward_kernel(mine, params, mask_ref, cot_in, pre_in, *refs, first, part_count):
    parts = refs[:part_count]
    grad_pre, sums, output, ordered, cot_ref, pre_ref, out_ref, sems, out_sems = refs[-9:]
    rows, span = grad_pre.shape
    step = rows // 4
    there = pl.ds(first, span)
    copies, sent = [], []
    for n in range(4):
        here = pl.ds(n * step, step)
        copies += [
            pltpu.make_async_copy(pre_in.at[here, :], pre_ref.at[here, :], sems.at[0, n]),
            pltpu.make_async_copy(cot_in.at[here, there], cot_ref.at[here, :], sems.at[1, n]),
        ]
    for copy in copies:
        copy.start()
    mean, spread, shift_grad, scale_sum, count = merged(mine[0], parts, ordered)
    inverse = lax.rsqrt(spread / count + NORM_EPS)
    scale_grad = scale_sum * inverse
    scale, shift = params[1:2, :], params[2:3, :]
    gain = scale * inverse
    shift_mean, scale_mean = shift_grad / count, scale_grad / count
    for i, row in enumerate((scale_grad, shift_grad)):
        sums[i + 1 : i + 2, :] = row[:, first : first + span]
    sums[3:8, :] = jnp.zeros((5, span), jnp.float32)
    for n in range(4):
        for copy in copies[2 * n : 2 * n + 2]:
            copy.wait()
        at = slice(n * step, (n + 1) * step)
        mask = mask_ref[at, :]
        for part in range(span // LANES):
            here = slice(part * LANES, (part + 1) * LANES)
            of = slice(first + part * LANES, first + (part + 1) * LANES)
            v = pre_ref[at, here]
            bend = gelu_parts(v)
            act = 0.5 * v * (1.0 + bend)
            normed = (act - mean[:, of]) * inverse[:, of]
            out_ref[at, here] = (mask * (scale[:, of] * normed + shift[:, of])).astype(jnp.bfloat16)
            grad_out = mask * cot_ref[at, here].astype(jnp.float32)
            grad_act = (
                mask * gain[:, of] * (grad_out - shift_mean[:, of] - normed * scale_mean[:, of])
            )
            slope = 0.5 * (1.0 + bend) + 0.5 * v * (1.0 - bend * bend) * (
                GELU_ROOT * (1.0 + 3.0 * GELU_CUBE * (v * v))
            )
            low = (grad_act * slope).astype(jnp.bfloat16)
            grad_pre[at, here] = low
            total = jnp.sum(low.astype(jnp.float32), axis=0, keepdims=True)
            sums[0:1, here] = total if n == 0 else sums[0:1, here] + total
        here = pl.ds(n * step, step)
        sent.append(
            pltpu.make_async_copy(out_ref.at[here, :], output.at[here, there], out_sems.at[n])
        )
        sent[-1].start()
    for copy in sent:
        copy.wait()


def backward(mine, params, mask, cotangent, preact, parts, part, output):
    rows, span = preact.shape
    width = cotangent.shape[1]
    before = [] if output is None else [output]

    def kernel(*refs):
        backward_kernel(*refs, first=part * span, part_count=len(parts))

    return call(
        kernel,
        flops=50 * rows * span,
        vmem_mb=62,
        in_specs=[SMEM, VMEM, VMEM, ANY, ANY] + [VMEM] * len(parts) + [ANY] * len(before),
        out_specs=[VMEM, VMEM, ANY],
        out_shape=[
            SDS((rows, span), jnp.bfloat16),
            SDS((STAT_ROWS, span), jnp.float32),
            SDS((rows, width), jnp.bfloat16),
        ],
        scratch_shapes=[
            pltpu.VMEM((len(parts), STAT_ROWS, width), jnp.float32),
            pltpu.VMEM((rows, span), jnp.bfloat16),
            pltpu.VMEM((rows, span), jnp.float32),
            pltpu.VMEM((rows, span), jnp.bfloat16),
            pltpu.SemaphoreType.DMA((2, 4)),
            pltpu.SemaphoreType.DMA((4,)),
        ],
        input_output_aliases={5 + len(parts): 2} if before else {},
        name="backward",
    )(mine[None], params, mask, cotangent, preact, *parts, *before)


def outers_kernel(me, *refs):
    inputs, outputs, buffers = list(refs[:6]), refs[6:10], refs[10:16]
    low_ref, sems, out_sems = refs[16:]
    inputs[0] = inputs[0].at[0]
    copies = [
        pltpu.make_async_copy(source, buffer, sems.at[n])
        for n, (source, buffer) in enumerate(zip(inputs, buffers))
    ]
    for copy in copies[:4]:
        copy.start()
    own_flip, near_flip = buffers[:2]
    rows, span = buffers[2].shape
    half = rows // 2
    sent = []
    for part in range(2):
        for n in ((0, 1, 2, 3), (4, 5))[part]:
            copies[n].wait()
        if part == 0:
            for copy in copies[4:]:
                copy.start()
        grad, near_grad = buffers[2 + 2 * part : 4 + 2 * part]
        for c in range(span // COLS):
            cs = slice(c * COLS, (c + 1) * COLS)
            total = dot(own_flip[...], grad[:, cs]) + dot(near_flip[...], near_grad[:, cs])
            low_ref[part, :, cs] = total.astype(jnp.bfloat16)
        for n in range(2):
            here = pl.ds(n * half, half)
            if part:
                kept, given = (
                    pl.multiple_of(n * rows + flag * half, half) for flag in (me[2], 1 - me[2])
                )
            else:
                kept, given = n * half, rows + n * half
            for m, start in enumerate((kept, given)):
                sent.append(
                    pltpu.make_async_copy(
                        low_ref.at[part, pl.ds(start, half), :],
                        outputs[2 * part + m].at[here, :],
                        out_sems.at[part, m, n],
                    )
                )
                sent[-1].start()
    for copy in sent:
        copy.wait()


def outers(me, hidden_flip, near_flip, grads, near_grads):
    rows, span = grads[0].shape
    low = jnp.bfloat16
    inputs = [hidden_flip, near_flip, grads[0], near_grads[0], grads[1], near_grads[1]]
    return call(
        outers_kernel,
        flops=0,
        vmem_mb=56,
        in_specs=[SMEM] + [ANY] * 6,
        out_specs=[ANY] * 4,
        out_shape=[SDS((rows, span), low)] * 4,
        scratch_shapes=[pltpu.VMEM(v.shape[-2:], low) for v in inputs]
        + [
            pltpu.VMEM((2, 2 * rows, span), low),
            pltpu.SemaphoreType.DMA((6,)),
            pltpu.SemaphoreType.DMA((2, 2, 2)),
        ],
        name="outers",
    )(me, *inputs)


def hidden_kernel(me, *refs, piece_total, slot_total, halved):
    inputs, refs = refs[: 3 + piece_total], refs[3 + piece_total :]
    outputs, refs = refs[: 1 + slot_total], refs[1 + slot_total :]
    buffers, refs = refs[: 3 + piece_total], refs[3 + piece_total :]
    grad_hidden, slots, sems, out_sem, slot_sems = refs
    grads, weights, halo_flip = buffers[:2], buffers[2:-1], buffers[-1]
    copies = [
        pltpu.make_async_copy(source, buffer, sems.at[n])
        for n, (source, buffer) in enumerate(zip(inputs, buffers))
    ]
    for copy in copies:
        copy.start()
    rows, width = grad_hidden.shape
    span = grads[0].shape[1]
    for copy in copies[:2]:
        copy.wait()
    for start, ref, copy in zip(weight_starts(me, rows), weights, copies[2:]):
        copy.wait()
        for c in range(ref.shape[0] // COLS):
            total = sum(
                dot(
                    grad[...],
                    ref[c * COLS : (c + 1) * COLS, p * span : (p + 1) * span],
                    BOTH_LAST,
                )
                for p, grad in enumerate(grads)
            )
            at = pl.multiple_of(start + c * COLS, COLS)
            grad_hidden[:, pl.ds(at, COLS)] = total.astype(jnp.bfloat16)
    out_copy = pltpu.make_async_copy(grad_hidden, outputs[0], out_sem)
    out_copy.start()
    copies[-1].wait()
    side = slots.shape[1] // SLOT_GROUP
    count = halo_flip.shape[0] // side - 1
    targets = list(outputs[1:])
    pending = {}
    for first in range(0, count, SLOT_GROUP):
        taken = min(SLOT_GROUP, count - first)
        buffer = first // SLOT_GROUP % 2
        for copy in pending.pop(buffer, ()):
            copy.wait()
        for c in range(width // COLS):
            cs = slice(c * COLS, (c + 1) * COLS)
            picked = halo_flip[(first + 1) * side : (first + 1 + taken) * side, :]
            slots[buffer, : taken * side, cs] = dot(picked, grad_hidden[:, cs]).astype(jnp.bfloat16)
        pending[buffer] = []
        for n in range(taken):
            for part in range(2 if first + n + 1 in halved else 1):
                target = targets.pop(0)
                height = target.shape[0]
                pending[buffer].append(
                    pltpu.make_async_copy(
                        slots.at[buffer, pl.ds(n * side + part * height, height), :],
                        target,
                        slot_sems.at[buffer, n, part],
                    )
                )
                pending[buffer][-1].start()
    for copy in sum(pending.values(), [out_copy]):
        copy.wait()


def hidden_grads(me, grads, weights, halo_flip, side, halved):
    rows, span = grads[0].shape
    width = 2 * span
    count = halo_flip.shape[0] // side - 1
    low = jnp.bfloat16
    shapes = []
    for k in range(1, count + 1):
        shapes += [SDS((side // 2, width), low)] * 2 if k in halved else [SDS((side, width), low)]
    inputs = [*grads, *weights, halo_flip]

    def kernel(*refs):
        hidden_kernel(*refs, piece_total=len(weights), slot_total=len(shapes), halved=halved)

    grad_hidden, *outs = call(
        kernel,
        flops=0,
        vmem_mb=56,
        in_specs=[SMEM] + [ANY] * len(inputs),
        out_specs=[ANY] * (1 + len(shapes)),
        out_shape=[SDS((rows, width), low)] + shapes,
        scratch_shapes=[pltpu.VMEM(v.shape, low) for v in inputs]
        + [
            pltpu.VMEM((rows, width), low),
            pltpu.VMEM((2 if count > SLOT_GROUP else 1, SLOT_GROUP * side, width), low),
            pltpu.SemaphoreType.DMA((len(inputs),)),
            pltpu.SemaphoreType.DMA,
            pltpu.SemaphoreType.DMA((2, SLOT_GROUP, 2)),
        ],
        name="hidden_grads",
    )(me, *inputs)
    slots = {}
    for k in range(1, count + 1):
        for part in range(2 if k in halved else 1):
            slots[k, part] = outs.pop(0)
    return grad_hidden, slots


def pieces_of(chooser, numbers, side):
    return [chooser[:, (k - 1) * side : k * side] for k in numbers]


def near_back(flips, grads, chooser, returned):
    rows, width = grads[0].shape
    numbers, blocks = sorted(returned), [returned[k] for k in sorted(returned)]
    side = blocks[0].shape[0]

    def kernel(*refs):
        flips_in, refs = refs[: len(flips)], refs[len(flips) :]
        grads_in, refs = refs[: len(grads)], refs[len(grads) :]
        chooser_ref, blocks_in, out = refs[0], refs[1:-1], refs[-1]
        picked = jnp.concatenate(pieces_of(chooser_ref, numbers, side), axis=1)
        for c in range(width // COLS):
            cs = slice(c * COLS, (c + 1) * COLS)
            total = dot(picked, jnp.concatenate([block[:, cs] for block in blocks_in], axis=0))
            done = 0
            for grad in grads_in:
                depth = grad.shape[0]
                flip = flips_in[done // rows]
                total += dot(flip[:, done % rows : done % rows + depth], grad[:, cs])
                done += depth
            out[:, cs] = total.astype(out.dtype)

    blocked = chooser.shape[1] > WHOLE_HALO
    if blocked:
        grid, block, whole = columns(width, True)
        specs = [whole((rows, rows))] * len(flips) + [block(g.shape[0]) for g in grads]
        specs += [whole(chooser.shape)] + [block(side)] * len(blocks)
        width = COLS
    else:
        grid, specs = {}, [VMEM] * (len(flips) + len(grads) + 1 + len(blocks))
    return call(
        kernel,
        flops=0,
        vmem_mb=56,
        in_specs=specs,
        out_specs=block(rows) if blocked else VMEM,
        out_shape=SDS((rows, grads[0].shape[1]), jnp.bfloat16),
        name="near_back",
        **grid,
    )(*flips, *grads, chooser, *blocks)


def give_back(chooser, base, returned):
    rows, width = base.shape
    numbers, blocks = sorted(returned), [returned[k] for k in sorted(returned)]
    side = blocks[0].shape[0]
    blocked = chooser.shape[1] > WHOLE_HALO
    grid, block, whole = columns(width, blocked)

    def kernel(chooser_ref, base_ref, *refs):
        blocks_in, out = refs[:-1], refs[-1]
        picked = jnp.concatenate(pieces_of(chooser_ref, numbers, side), axis=1)
        for c in range(out.shape[1] // COLS):
            cs = slice(c * COLS, (c + 1) * COLS)
            pieces = jnp.concatenate([block[:, cs] for block in blocks_in], axis=0)
            out[:, cs] = (base_ref[:, cs].astype(jnp.float32) + dot(picked, pieces)).astype(jnp.bfloat16)

    return call(
        kernel,
        flops=0,
        vmem_mb=56,
        in_specs=[whole(chooser.shape), block(rows)] + [block(side)] * len(blocks),
        out_specs=block(rows),
        out_shape=SDS((rows, width), jnp.bfloat16),
        name="give_back",
        **grid,
    )(chooser, base, *blocks)


def lamb_step(value, grad, first, second, decay):
    first_new = DECAY_FIRST * first + (1.0 - DECAY_FIRST) * grad
    second_new = DECAY_SECOND * second + (1.0 - DECAY_SECOND) * grad * grad
    update = (
        first_new
        / (1.0 - DECAY_FIRST**STEP)
        / (jnp.sqrt(second_new / (1.0 - DECAY_SECOND**STEP)) + ADAM_EPS)
        + decay * value
    )
    return (first_new, second_new, update)


def term_sum(terms):
    return sum(term[...].astype(jnp.float32) for term in terms)


def first_sends(side_bit, keep_a, came_a, keep_b, came_b):
    rows, span = keep_a.shape
    half = rows // 2
    block = lambda place: pl.BlockSpec((half, span), place)
    other, second = block(lambda i, bit: (1 - bit[0], 0)), block(lambda i, bit: (1, 0))

    def kernel(bit, *refs):
        for n, out in enumerate(refs[4:]):
            out[...] = term_sum(refs[2 * n : 2 * n + 2]).astype(out.dtype)

    return call(
        kernel,
        flops=0,
        vmem_mb=56,
        grid_spec=pltpu.PrefetchScalarGridSpec(
            num_scalar_prefetch=1,
            grid=(1,),
            in_specs=[other] * 2 + [second] * 2,
            out_specs=[block(lambda i, bit: (0, 0))] * 2,
        ),
        out_shape=[SDS((half, span), jnp.bfloat16)] * 2,
        name="first_sends",
    )(side_bit[None], keep_a, came_a, keep_b, came_b)


def rows_sum(start, rows, terms_a, terms_b, terms, extra=()):
    span = terms_a[0][0].shape[1]
    narrow = [*terms_a, *terms_b]
    places = jnp.stack([(start - offset) // rows for _, offset in [*narrow, *terms]]).astype(jnp.int32)
    at = lambda n, cols: pl.BlockSpec((rows, cols), lambda i, places: (places[n], 0))
    specs = [at(n, span) for n in range(len(narrow))]
    specs += [at(len(narrow) + n, 2 * span) for n in range(len(terms))]
    return places, specs, [term for term, _ in [*narrow, *terms]], len(terms_a), len(narrow)


def send_rows(start, rows, terms_a, terms_b, terms):
    places, specs, arrays, cut, narrow = rows_sum(start, rows, terms_a, terms_b, terms)
    span = arrays[0].shape[1]

    def kernel(places, *refs):
        out = refs[-1]
        wide = term_sum(refs[narrow:-1])
        for n, part in enumerate((refs[:cut], refs[cut:narrow])):
            cs = slice(n * span, (n + 1) * span)
            more = wide if isinstance(wide, int) else wide[:, cs]
            out[:, cs] = (term_sum(part) + more).astype(out.dtype)

    return call(
        kernel,
        flops=0,
        vmem_mb=56,
        grid_spec=pltpu.PrefetchScalarGridSpec(
            num_scalar_prefetch=1,
            grid=(1,),
            in_specs=specs,
            out_specs=pl.BlockSpec((rows, 2 * span), lambda i, places: (0, 0)),
        ),
        out_shape=SDS((rows, 2 * span), jnp.bfloat16),
        name="send_rows",
    )(places, *arrays)


def piece_totals(start, rows, terms_a, terms_b, terms, sums, weight, first, second):
    places, specs, arrays, cut, narrow = rows_sum(start, rows, terms_a, terms_b, terms)
    span = arrays[0].shape[1]
    own = pl.BlockSpec((rows, 2 * span), lambda i, places: (places[0], 0))
    whole = lambda height: pl.BlockSpec((height, 2 * span), lambda i, places: (0, 0))

    def kernel(places, *refs):
        sums, value, first, second, piece, totals = refs[-6:]
        wide = term_sum(refs[narrow:-6])
        totals[0:1, :] = sums[0:1, :]
        totals[3:8, :] = jnp.zeros((5, 2 * span), jnp.float32)
        for n, part in enumerate((refs[:cut], refs[cut:narrow])):
            cs = slice(n * span, (n + 1) * span)
            low = (term_sum(part) + wide[:, cs]).astype(jnp.bfloat16)
            piece[:, cs] = low
            update = lamb_step(
                value[:, cs], low.astype(jnp.float32), first[:, cs], second[:, cs], WEIGHT_DECAY
            )[2]
            totals[1:2, cs] = jnp.sum(value[:, cs] * value[:, cs], axis=0, keepdims=True)
            totals[2:3, cs] = jnp.sum(update * update, axis=0, keepdims=True)

    return call(
        kernel,
        flops=0,
        vmem_mb=56,
        grid_spec=pltpu.PrefetchScalarGridSpec(
            num_scalar_prefetch=1,
            grid=(1,),
            in_specs=specs + [whole(STAT_ROWS)] + [own] * 3,
            out_specs=[whole(rows), whole(STAT_ROWS)],
        ),
        out_shape=[SDS((rows, 2 * span), jnp.bfloat16), SDS((STAT_ROWS, 2 * span), jnp.float32)],
        name="piece_totals",
    )(places, *arrays, sums, weight, first, second)


def by_bit(flag, own, came):
    rows, width = own.shape
    mine = (jnp.arange(2, dtype=jnp.int32) == flag)[:, None, None]
    return jnp.where(mine, own[None], came[None]).reshape(2 * rows, width)


def on_device(
    features,
    adjacency,
    tile_values,
    tile_block,
    tile_slot,
    tile_count,
    send_block,
    node_mask,
    weight,
    params,
    weight_first,
    weight_second,
    params_first,
    params_second,
    cotangent,
):
    dom_count, row_count = lax.axis_size("dom"), lax.axis_size("row")
    dom_at, row_at = lax.axis_index("dom"), lax.axis_index("row")
    rows, width = features.shape
    side = tile_values.shape[1]
    side_bit = dom_at % 2
    me = jnp.stack([dom_at, row_at, side_bit]).astype(jnp.int32)
    sends = send_block[0]
    mask = jnp.broadcast_to(node_mask.astype(jnp.float32)[:, None], (rows, LANES))

    half = rows // 2
    low_weight = weight.astype(jnp.bfloat16)
    first_half, second_half, blocks = outgoing(me, sends, features, side)
    wide, flip, halo, halo_flip, chooser = prepare(
        me, sends, tile_block, tile_slot, tile_count, adjacency, tile_values, dom_count
    )

    far, light = turns(dom_count)
    arrived = {}
    whole = lambda order: [(k, 0) for k in order]
    out = lambda key: blocks[key[0] - 1]
    far_first = swap(first_half, 0, 2)
    near_features = swap(features, 0, 1)
    turn = [
        far_first,
        near_features,
        send_in_turn(out, whole(far[0]), arrived),
        send_in_turn(out, whole(light[0]), arrived),
    ]
    far_second = swap(hold(second_half, *turn), 0, 2)
    cross = [swap(hold(far_first, *turn), 0, 1)]
    turn = [
        far_second,
        cross[0],
        send_in_turn(out, whole(far[1]), arrived, *turn),
        send_in_turn(out, whole(light[1]), arrived, *turn),
    ]
    over_y = swap(hold(low_weight[:half], *turn), 0, 2)
    cross.append(swap(hold(far_second, *turn), 0, 1))
    near_weight = swap(hold(low_weight, *turn), 0, 1)
    turn = [
        over_y,
        cross[1],
        near_weight,
        send_in_turn(out, whole(far[2]), arrived, *turn),
        send_in_turn(out, whole(light[2]), arrived, *turn),
    ]
    over_y_too = swap(hold(low_weight[half:], *turn), 0, 2)
    send_in_turn(out, whole(far[3]), arrived, *turn)
    base = near(wide, [features, near_features, far_first, far_second] + cross)
    weights = [
        low_weight,
        near_weight,
        over_y,
        over_y_too,
        swap(hold(over_y, base), 0, 1),
        swap(over_y_too, 0, 1),
    ]
    arrived = [arrived[k, 0] for k in range(1, dom_count)]
    hidden, hidden_flip = add_halo(me, base, halo, arrived, row_count)
    pre_first, pre_second, stats = linear(me, hidden, params, mask, cotangent, weights)
    mine, parts = exchange_stats(stats, dom_at, row_at, dom_count, row_count)
    near_flip = swap(hidden_flip[1], 0, 1)

    mine = hold(mine, near_flip)
    output, grads, near_pre, sums = None, [], [], []
    for part, preact in enumerate((pre_first, pre_second)):
        grad_pre, sum_part, output = backward(
            mine, params, mask, cotangent, preact, parts, part, output
        )
        grads.append(grad_pre)
        near_pre.append(swap(grad_pre, 0, 1))
        sums.append(sum_part)
    sums = jnp.concatenate(sums, axis=1)
    halved = []
    keep_a, send_a, keep_b, send_b = outers(me, hidden_flip, near_flip, grads, near_pre)
    grad_hidden, slots = hidden_grads(me, grads, weights, halo_flip, side, halved)

    returned = {}
    part_of = lambda order, n: [(k, n) for k in order]
    bit = lambda step: (dom_at // step) % 2
    blocks_back = lambda order, *turn: send_in_turn(lambda k: slots[k], order, returned, *turn)

    turn_flip = lambda j, *turn: swap(hold(flip[j * rows : (j + 1) * rows], *turn), 0, j)
    rounds = groups(dom_count, row_count)

    small_steps = sum(rounds, [])

    flips = [flip[:rows], turn_flip(1, send_a), None, None]
    turn = [swap(send_a, 0, 2), swap(send_b, 1, 0), flips[1], grad_hidden]
    sent_a, sent_b = first_sends(side_bit, keep_a, turn[0], keep_b, turn[1])
    terms_a, terms_b, terms = [(keep_a, 0), (turn[0], 0)], [(keep_b, side_bit * half), (turn[1], side_bit * half)], []
    near_grad = swap(hold(grad_hidden, *turn), 0, 1)
    flips[2] = turn_flip(2, *turn)
    turn = [
        swap(hold(sent_a, *turn), 1, 0),
        swap(hold(sent_b, *turn), 0, 2),
        blocks_back(whole(far[0]), *turn),
        near_grad,
        flips[2],
    ]
    first, span = side_bit * half, half
    terms_a.append((turn[0], first))
    terms_b.append((turn[1], first))
    steps = [1 << n for n in range(1, dom_count.bit_length() - 1)]
    quarter = rows // 4
    grad_parts, cross = [], []

    def over_y_back(*turn):
        n = len(grad_parts)
        grad_parts.append(
            swap(hold(grad_hidden[n * quarter : (n + 1) * quarter], *turn), 0, 2)
        )
        more = [grad_parts[n]]
        if n > 1:
            cross.append(swap(hold(grad_parts[n - 2], *turn), 0, 1))
            more.append(cross[n - 2])
        if n == 1:
            flips[3] = turn_flip(3, *turn)
            more.append(flips[3])
        return more

    beside = [
        [whole(far[2]), whole(light[0])],
        [whole(light[1])],
        [],
        [whole(far[3])],
    ]
    for n, step in enumerate(steps):
        span //= 2
        sent = send_rows(first + (1 - bit(step)) * span, span, terms_a, terms_b, terms)
        first = first + bit(step) * span
        came = swap(hold(sent, *turn), step, 0)
        terms.append((came, first))
        more = []
        if n < 2:
            more = [blocks_back(order, *turn) for order in beside[n]] + over_y_back(*turn)
        turn = [came] + more
    weight_grad, totals = piece_totals(
        first, span, terms_a, terms_b, terms, sums, weight, weight_first, weight_second
    )
    for n, step in enumerate(reversed(steps)):
        came = swap(hold(weight_grad, *turn), step, 0)
        more = []
        if n < 2:
            more = [blocks_back(order, *turn) for order in beside[2 + n]] + over_y_back(*turn)
            for flip_bits in small_steps[:3] if n == 0 else small_steps[3:]:
                totals = pair_sum(totals, [flip_bits], *turn)
            more.append(totals)
        weight_grad = by_bit(bit(step), weight_grad, came)
        turn = [came] + more
    came = swap(hold(weight_grad, *turn), 1, 0)
    blocks_back(whole(far[1]), *turn)
    blocks_back(whole(light[2]), *turn)
    cross += [swap(hold(part, *turn), 0, 1) for part in grad_parts[-2:]]
    bias_grad = totals[0:1]
    weight_norms = jnp.sqrt(jnp.sum(totals[1:3], axis=1))
    late = far[1] + light[2]
    base = near_back(
        flips,
        [grad_hidden, near_grad] + grad_parts + cross,
        chooser,
        {key[0]: value for key, value in returned.items() if key[0] not in late},
    )
    weight_grad = by_bit(bit(1), weight_grad, hold(came, base)).astype(jnp.float32)
    returned = {key[0]: value for key, value in returned.items() if key[0] in late}
    weight_first_new, weight_second_new, weight_update = lamb_step(
        weight, weight_grad, weight_first, weight_second, WEIGHT_DECAY
    )
    weight_new = (
        weight - LEARN_RATE * (weight_norms[0] / (weight_norms[1] + TRUST_EPS)) * weight_update
    )

    grad_features = give_back(chooser, hold(base, weight_new), returned)
    param_grads = jnp.concatenate([bias_grad, sums[1:3]], axis=0)
    params_first_new, params_second_new, param_update = lamb_step(
        params, param_grads, params_first, params_second, 0.0
    )
    param_norms = jnp.sqrt(jnp.sum(params * params, axis=1, keepdims=True))
    update_norms = jnp.sqrt(jnp.sum(param_update * param_update, axis=1, keepdims=True))
    params_new = params - LEARN_RATE * (param_norms / (update_norms + TRUST_EPS)) * param_update
    norms = jnp.concatenate(
        [weight_norms[None, :], jnp.concatenate([param_norms, update_norms], axis=1)], axis=0
    )
    return (
        output,
        grad_features,
        weight_new,
        weight_new.astype(jnp.bfloat16),
        weight_first_new,
        weight_second_new,
        params_new,
        params_first_new,
        params_second_new,
        norms,
    )


def solution(mesh):
    in_specs = (
        P(("dom", "row"), None),
        P(("dom", "row"), None),
        P(("dom", "row"), None, None),
        P(("dom", "row")),
        P(("dom", "row")),
        P(("dom", "row")),
        P(("dom", "row"), None),
        P(("dom", "row")),
        P("row", None),
        P(),
        P("row", None),
        P("row", None),
        P(),
        P(),
        P(("dom", "row"), None),
    )
    out_specs = (
        P(("dom", "row"), None),
        P(("dom", "row"), None),
        P("row", None),
        P("row", None),
        P("row", None),
        P("row", None),
        P(),
        P(),
        P(),
        P(),
    )
    return jax.shard_map(
        on_device, mesh=mesh, in_specs=in_specs, out_specs=out_specs, check_vma=False
    )
```
